512 devices in a mesh: gx: 8 (over z_hi, x), gy: 64 (over y, z_lo, core).
Axes of the slice: x: 4, y: 4, z: 16 (z_hi: 2, z_lo: 8; z = z_hi * 8 + z_lo), core: 2. Of those that a mesh axis runs over, the one named last changes fastest.
Arguments:
- grid_latent: bfloat16 [16, 4096, 512], P('gx', 'gy'), may hold values from -6 to 6
- mesh_latent: bfloat16 [8, 64, 256, 512], P('gx', 'gy'), may hold values from -6 to 6
- encode_message: bfloat16 [512, 512], replicated, may hold values from -0.25 to 0.25
- encode_update: bfloat16 [512, 512], replicated, may hold values from -0.25 to 0.25
- process_message: bfloat16 [512, 512], replicated, may hold values from -0.25 to 0.25
- process_update: bfloat16 [512, 512], replicated, may hold values from -0.25 to 0.25
- decode_message: bfloat16 [512, 512], replicated, may hold values from -0.25 to 0.25
- decode_update: bfloat16 [512, 512], replicated, may hold values from -0.25 to 0.25
- encode_source: int32 [8, 64, 1024], P('gx', 'gy'), may hold values from 0 to 65535, as said below
- encode_target: int32 [8, 64, 1024], P('gx', 'gy'), may hold values from -1 to 255, as said below
- process_source: int32 [8, 64, 1024], P('gx', 'gy'), may hold values from 0 to 255
- process_target: int32 [8, 64, 1024], P('gx', 'gy'), may hold values from -1 to 255, as said below
- decode_source: int32 [8, 64, 1024], P('gx', 'gy'), may hold values from 0 to 131071, as said below
- decode_target: int32 [8, 64, 1024], P('gx', 'gy'), may hold values from -1 to 127
Outputs:
- grid_output: bfloat16 [16, 4096, 512], P('gx', 'gy')
- mesh_output: bfloat16 [8, 64, 256, 512], P('gx', 'gy')
The draws below stay inside these ranges and needn't reach their ends.
Inputs may be any that keep to these rules, and one draw needn't show every extreme that they name: `encode_source`: the source of a slot of band b and sector s lies in grid rows b * 2 - 1 to (b + 1) * 2 and in the 80 columns from s * 64 - 8, modulo 4096. `encode_target`: every slot of the first and the last band is live. `process_target`: slots whose source sector is the device's own sector or one next to it (with wrapping) are all live. `decode_source`: the source of a slot of band b and sector s lies in band b and in sectors s - 1, s or s + 1, modulo 64.
All inputs are finite; a program needn't handle non-finite values.
Results may differ from the reference program's by a relative error of at most 0.008.
Values may be sent and summed in bfloat16 or wider, within the bound.
No kernel may reach another device: no remote copies, remote signals or barrier semaphores. Data moves between devices by JAX's collectives and lax.ppermute only.
A program may use at most 64 MiB of HBM per device.

```python
import jax
import jax.numpy as jnp
from jax import lax

D = 512
LAT_DEV = 2
LON_DEV = 64
HALO = 8
MESH_DEV = 256
ENC_DEV = 1024
MEDGE_DEV = 1024
DEC_DEV = 1024
BANDS = 8
SECTORS = 64
LAT = 16
LON = 4096
CAP = 16


def draw_encode_source(key, part):
    key = jax.random.fold_in(key, 11)
    shape = (BANDS, SECTORS, ENC_DEV)
    band = lax.broadcasted_iota(jnp.int32, shape, 0)
    sector = lax.broadcasted_iota(jnp.int32, shape, 1)
    lat_key, lon_key = jax.random.split(key)
    lat_step = jax.random.randint(lat_key, shape, -1, LAT_DEV + 1)
    lon_step = jax.random.randint(lon_key, shape, -HALO, LON_DEV + HALO)
    latitude = jnp.clip(band * LAT_DEV + lat_step, 0, LAT - 1)
    longitude = (sector * LON_DEV + lon_step) % LON
    return (latitude * LON + longitude).astype(jnp.int32)


def draw_encode_target(key, part):
    key = jax.random.fold_in(key, 12)
    shape = (BANDS, SECTORS, ENC_DEV)
    band = lax.broadcasted_iota(jnp.int32, shape, 0)
    node_key, live_key = jax.random.split(key)
    target = jax.random.randint(node_key, shape, 0, MESH_DEV)
    distance = jnp.abs(2 * band - (BANDS - 1))
    live = jax.random.randint(live_key, shape, 0, 2 * (BANDS - 1)) < BANDS - 1 + distance
    return jnp.where(live, target, -1).astype(jnp.int32)


def draw_process_source(key, part):
    key = jax.random.fold_in(key, 13)
    shape = (BANDS, SECTORS, MEDGE_DEV)
    return jax.random.randint(key, shape, 0, MESH_DEV).astype(jnp.int32)


def draw_process_target(key, part):
    key = jax.random.fold_in(key, 14)
    shape = (BANDS, SECTORS, MEDGE_DEV)
    sector = lax.broadcasted_iota(jnp.int32, shape, 1)
    owner = lax.broadcasted_iota(jnp.int32, shape, 2) // CAP
    distance = jnp.minimum((owner - sector) % SECTORS, (sector - owner) % SECTORS)
    node_key, live_key = jax.random.split(key)
    target = jax.random.randint(node_key, shape, 0, MESH_DEV)
    live = (distance <= 1) | (jax.random.randint(live_key, shape, 0, 2) == 1)
    return jnp.where(live, target, -1).astype(jnp.int32)


def draw_decode_source(key, part):
    key = jax.random.fold_in(key, 15)
    shape = (BANDS, SECTORS, DEC_DEV)
    band = lax.broadcasted_iota(jnp.int32, shape, 0)
    sector = lax.broadcasted_iota(jnp.int32, shape, 1)
    step_key, row_key = jax.random.split(key)
    step = jax.random.randint(step_key, shape, -1, 2)
    source_sector = (sector + step) % SECTORS
    row = jax.random.randint(row_key, shape, 0, MESH_DEV)
    return ((band * SECTORS + source_sector) * MESH_DEV + row).astype(jnp.int32)


def draw_decode_target(key, part):
    key = jax.random.fold_in(key, 16)
    shape = (BANDS, SECTORS, DEC_DEV)
    node_key, live_key = jax.random.split(key)
    target = jax.random.randint(node_key, shape, 0, LAT_DEV * LON_DEV)
    live = jax.random.randint(live_key, shape, 0, 4) < 3
    return jnp.where(live, target, -1).astype(jnp.int32)


def block_scale(key, extent, cuts, least, top_value):
    def one(axis_at, parts):
        heights = jax.random.uniform(jax.random.fold_in(jax.random.fold_in(key, 6), axis_at), (parts,), jnp.float32, least / len(cuts), top_value / len(cuts))
        return jnp.repeat(jnp.exp(heights), extent[axis_at] // parts).reshape((-1,) + (1,) * (len(extent) - axis_at - 1))

    level = one(*cuts[0])
    for cut in cuts[1:]:
        level = level * one(*cut)
    return level


def centred(key, dims, scale, bound, shards=(), kind=jnp.bfloat16):
    gain = block_scale(key, dims, shards, -0.22, 0.18) if shards else 1.0
    values = jax.random.normal(key, dims, jnp.float32) * scale * gain
    return jnp.minimum(jnp.maximum(values, -bound), bound).astype(kind)


def setup_inputs(seed: int = 0) -> dict:
    splits = jax.random.split(jax.random.key(seed), 15)
    return {
        "grid_latent": centred(splits[0], (LAT, LON, D), 1.0, 6.0, ((0, 8), (1, 64))),
        "mesh_latent": centred(splits[1], (BANDS, SECTORS, MESH_DEV, D), 1.0, 6.0, ((0, 8), (1, 64))),
        "encode_message": centred(splits[2], (D, D), D ** -0.5, 0.25),
        "encode_update": centred(splits[3], (D, D), D ** -0.5, 0.25),
        "process_message": centred(splits[4], (D, D), D ** -0.5, 0.25),
        "process_update": centred(splits[5], (D, D), D ** -0.5, 0.25),
        "decode_message": centred(splits[6], (D, D), D ** -0.5, 0.25),
        "decode_update": centred(splits[7], (D, D), D ** -0.5, 0.25),
        "encode_source": draw_encode_source(jax.random.fold_in(splits[14], 71), 0),
        "encode_target": draw_encode_target(jax.random.fold_in(splits[14], 71), 0),
        "process_source": draw_process_source(jax.random.fold_in(splits[14], 71), 0),
        "process_target": draw_process_target(jax.random.fold_in(splits[14], 71), 0),
        "decode_source": draw_decode_source(jax.random.fold_in(splits[14], 71), 0),
        "decode_target": draw_decode_target(jax.random.fold_in(splits[14], 71), 0),
    }


EPSILON = 1e-05

def edge_messages(rows, targets):
    summed = rows.astype(jnp.float32) + targets.astype(jnp.float32)
    return jax.nn.silu(summed).astype(jnp.bfloat16)

def refresh(latent, summed, weight):
    scaled = summed * lax.rsqrt(lax.optimization_barrier(jnp.mean(summed * summed, axis=-1, keepdims=True)) + EPSILON)
    branch = jnp.dot(scaled.astype(jnp.bfloat16), weight, preferred_element_type=jnp.float32)
    return (latent.astype(jnp.float32) + branch).astype(jnp.bfloat16)

def band_sum(table, targets, source, target_index, count):
    live = target_index >= 0
    clamped = jnp.where(live, target_index, 0)
    messages = edge_messages(table[source], targets[clamped])
    messages = lax.optimization_barrier(messages)
    slots = jnp.where(live, target_index, count)
    return jax.ops.segment_sum(messages.astype(jnp.float32), slots, num_segments=count + 1)[:count]

def reference(grid_latent, mesh_latent, encode_message, encode_update, process_message, process_update, decode_message, decode_update, encode_source, encode_target, process_source, process_target, decode_source, decode_target):
    grid_flat = grid_latent.reshape(LAT * LON, D)
    grid_table = jnp.dot(grid_flat, encode_message, preferred_element_type=jnp.float32).astype(jnp.bfloat16)
    mesh_bands = mesh_latent.reshape(BANDS, SECTORS * MESH_DEV, D)
    sector_ids = jnp.arange(SECTORS, dtype=jnp.int32)[:, None]
    band_count = SECTORS * MESH_DEV

    def encode_band(inputs):
        band_mesh, band_source, band_target = inputs
        offsets = jnp.where(band_target >= 0, band_target + sector_ids * MESH_DEV, -1).reshape(-1)
        summed = band_sum(grid_table, band_mesh, band_source.reshape(-1), offsets, band_count)
        return refresh(band_mesh, summed, encode_update)
    mesh_first = lax.map(encode_band, (mesh_bands, encode_source, encode_target))

    def process_band(inputs):
        band_mesh, band_source, band_target = inputs
        table = jnp.dot(band_mesh, process_message, preferred_element_type=jnp.float32).astype(jnp.bfloat16)
        owners = jnp.arange(MEDGE_DEV, dtype=jnp.int32)[None, :] // CAP
        rows = (owners * MESH_DEV + band_source).reshape(-1)
        offsets = jnp.where(band_target >= 0, band_target + sector_ids * MESH_DEV, -1).reshape(-1)
        summed = band_sum(table, band_mesh, rows, offsets, band_count)
        return refresh(band_mesh, summed, process_update)
    mesh_second = lax.map(process_band, (mesh_first, process_source, process_target))
    grid_bands = grid_latent.reshape(BANDS, LAT_DEV * LON, D)
    band_numbers = jnp.arange(BANDS, dtype=jnp.int32)

    def decode_band(inputs):
        band_mesh, band_grid, band_source, band_target, band_number = inputs
        table = jnp.dot(band_mesh, decode_message, preferred_element_type=jnp.float32).astype(jnp.bfloat16)
        rows = (band_source - band_number * band_count).reshape(-1)
        flat_targets = band_target // LON_DEV * LON + sector_ids * LON_DEV + band_target % LON_DEV
        offsets = jnp.where(band_target >= 0, flat_targets, -1).reshape(-1)
        summed = band_sum(table, band_grid, rows, offsets, LAT_DEV * LON)
        return refresh(band_grid, summed, decode_update)
    grid_new = lax.map(decode_band, (mesh_second, grid_bands, decode_source, decode_target, band_numbers))
    return (grid_new.reshape(LAT, LON, D), mesh_second.reshape(BANDS, SECTORS, MESH_DEV, D))
```

```python
import jax
import jax.numpy as jnp
from jax import lax
from jax.experimental import pallas as pl
from jax.experimental.pallas import tpu as pltpu
from jax.sharding import PartitionSpec as P

HALO = 8
EPSILON = 1e-05
LANES = 128
CHUNK = 256


def column(index, rows):
    parts = []
    for i in range(rows.start // LANES, rows.stop // LANES):
        row = jnp.broadcast_to(index[i : i + 1, :], (LANES, LANES))
        parts.append(row.T)
    return jnp.concatenate(parts, axis=0)


def pick(col, count):
    lane = lax.broadcasted_iota(jnp.int32, col.shape, 1)
    parts = [
        jnp.where(col == lane + k, 1.0, 0.0).astype(jnp.bfloat16)
        for k in range(0, count, LANES)
    ]
    return jnp.concatenate(parts, axis=1)


def spread(index, count):
    sub = lax.broadcasted_iota(jnp.int32, (count, LANES), 0)
    parts = [
        jnp.where(index[i : i + 1, :] == sub, 1.0, 0.0).astype(jnp.bfloat16)
        for i in range(index.shape[0])
    ]
    return jnp.concatenate(parts, axis=1)


def dot(a, b):
    return jnp.dot(a, b, preferred_element_type=jnp.float32)


def message(summed):
    half = 0.5 * summed
    return (half * jnp.tanh(half) + half).astype(jnp.bfloat16)


def refresh(latent, summed, weight):
    scaled = summed * lax.rsqrt(jnp.mean(summed * summed, axis=-1, keepdims=True) + EPSILON)
    return (latent.astype(jnp.float32) + dot(scaled.astype(jnp.bfloat16), weight)).astype(
        jnp.bfloat16
    )


def encode_kernel(
    grid, up, down, left, right, mesh, w_message, w_update, w_next,
    source, target, request, first_out, send_out, table, messages,
):
    w = w_message[...]
    cells = up.shape[0]
    inner = grid.shape[0]
    edge = left.shape[0]
    at = 0
    for ref, rows in ((up, cells), (grid, inner), (down, cells), (left, edge), (right, edge)):
        table[at : at + rows, :] = dot(ref[...], w).astype(jnp.bfloat16)
        at += rows
    pad = table.shape[0] - at
    table[at:, :] = jnp.zeros((pad, table.shape[1]), jnp.bfloat16)
    latent = mesh[...]
    nodes = latent.shape[0]
    src, tgt, req = source[...], target[...], request[...]
    edges = src.shape[0] * LANES
    for c in range(0, edges, CHUNK):
        rows = slice(c, c + CHUNK)
        acc = dot(pick(column(src, rows), table.shape[0]), table[...])
        acc = acc + dot(pick(column(tgt, rows), nodes), latent)
        messages[rows, :] = message(acc)
    summed = dot(spread(tgt, nodes), messages[...])
    first = refresh(latent, summed, w_update[...])
    first_out[...] = first
    following = dot(first, w_next[...]).astype(jnp.bfloat16)
    for c in range(0, edges, CHUNK):
        rows = slice(c, c + CHUNK)
        send_out[rows, :] = dot(pick(column(req, rows), nodes), following).astype(jnp.bfloat16)


def process_kernel(
    picked, first, w_update, w_next, target, second_out, table_out, messages
):
    latent = first[...]
    nodes = latent.shape[0]
    tgt = target[...]
    edges = tgt.shape[0] * LANES
    for c in range(0, edges, CHUNK):
        rows = slice(c, c + CHUNK)
        acc = dot(pick(column(tgt, rows), nodes), latent)
        messages[rows, :] = message(acc + picked[rows, :].astype(jnp.float32))
    summed = dot(spread(tgt, nodes), messages[...])
    second = refresh(latent, summed, w_update[...])
    second_out[...] = second
    table_out[...] = dot(second, w_next[...]).astype(jnp.bfloat16)


def decode_kernel(
    own, mate, other, grid, w_update, source, target, grid_out, messages
):
    latent = grid[...]
    cells = latent.shape[0]
    nodes = own.shape[0]
    src, tgt = source[...], target[...]
    edges = src.shape[0] * LANES
    for c in range(0, edges, CHUNK):
        rows = slice(c, c + CHUNK)
        col = column(src, rows)
        acc = dot(pick(column(tgt, rows), cells), latent)
        for at, ref in ((0, own), (nodes, mate), (2 * nodes, other)):
            acc = acc + dot(pick(col - at, nodes), ref[...])
        messages[rows, :] = message(acc)
    summed = dot(spread(tgt, cells), messages[...])
    grid_out[...] = refresh(latent, summed, w_update[...])


def on_device(
    grid_latent,
    mesh_latent,
    encode_message,
    encode_update,
    process_message,
    process_update,
    decode_message,
    decode_update,
    encode_source,
    encode_target,
    process_source,
    process_target,
    decode_source,
    decode_target,
):
    lat_rows, lon_cols, width = grid_latent.shape
    bands = lax.axis_size("gx")
    sectors = lax.axis_size("gy")
    lon_total = lon_cols * sectors
    band = lax.axis_index("gx")
    sector = lax.axis_index("gy")
    mesh_rows = mesh_latent.reshape(-1, width)
    nodes = mesh_rows.shape[0]
    grid_rows = grid_latent.reshape(-1, width)
    cells = grid_rows.shape[0]
    edges = encode_source.size
    bf16 = jnp.bfloat16
    params = pltpu.CompilerParams(vmem_limit_bytes=40 * 1024 * 1024)

    request = lax.all_to_all(
        process_source.reshape(sectors, -1), "gy", 0, 0, tiled=True
    ).reshape(-1, LANES)

    above = [(i, i + 1) for i in range(bands - 1)]
    below = [(i + 1, i) for i in range(bands - 1)]
    up = lax.ppermute(grid_latent[lat_rows - 1], "gx", above)
    down = lax.ppermute(grid_latent[0], "gx", below)
    tall = jnp.concatenate([up[None], grid_latent, down[None]])
    east = [(i, (i + 1) % sectors) for i in range(sectors)]
    west = [((i + 1) % sectors, i) for i in range(sectors)]
    left = lax.ppermute(tall[:, lon_cols - HALO :], "gy", east).reshape(-1, width)
    right = lax.ppermute(tall[:, :HALO], "gy", west).reshape(-1, width)

    source = encode_source.reshape(-1, LANES)
    lat = source // lon_total - band * lat_rows + 1
    lon = (source % lon_total - sector * lon_cols + HALO) % lon_total
    tall_cells = (lat_rows + 2) * lon_cols
    side = (lat_rows + 2) * HALO
    row = jnp.where(
        lon < HALO,
        tall_cells + lat * HALO + lon,
        jnp.where(
            lon < HALO + lon_cols,
            lat * lon_cols + lon - HALO,
            tall_cells + side + lat * HALO + lon - HALO - lon_cols,
        ),
    )
    depth = -(-(tall_cells + 2 * side) // LANES) * LANES
    first, send = pl.pallas_call(
        encode_kernel,
        out_shape=(
            jax.ShapeDtypeStruct((nodes, width), bf16),
            jax.ShapeDtypeStruct((edges, width), bf16),
        ),
        scratch_shapes=[pltpu.VMEM((depth, width), bf16), pltpu.VMEM((edges, width), bf16)],
        compiler_params=params,
    )(
        grid_rows, up, down, left, right, mesh_rows, encode_message, encode_update,
        process_message, row, encode_target.reshape(-1, LANES), request,
    )
    picked = lax.all_to_all(
        send.reshape(sectors, -1, width), "gy", 0, 0, tiled=True
    ).reshape(edges, width)
    second, table = pl.pallas_call(
        process_kernel,
        out_shape=(
            jax.ShapeDtypeStruct((nodes, width), bf16),
            jax.ShapeDtypeStruct((nodes, width), bf16),
        ),
        scratch_shapes=[pltpu.VMEM((edges, width), bf16)],
        compiler_params=params,
    )(picked, first, process_update, decode_message, process_target.reshape(-1, LANES))

    partner = [i + 1 if i % 2 else i - 1 for i in range(sectors)]
    other = lax.ppermute(table, "gy", [(i, partner[i] % sectors) for i in range(sectors)])
    mate = lax.ppermute(table, "gy", [(i, i ^ 1) for i in range(sectors)])
    source = decode_source.reshape(-1, LANES)
    owner = source // nodes % sectors
    piece = jnp.where(owner == sector, 0, jnp.where(owner == sector ^ 1, 1, 2))
    row = piece * nodes + source % nodes
    grid_output = pl.pallas_call(
        decode_kernel,
        out_shape=jax.ShapeDtypeStruct((cells, width), bf16),
        scratch_shapes=[pltpu.VMEM((edges, width), bf16)],
        compiler_params=params,
    )(table, mate, other, grid_rows, decode_update, row, decode_target.reshape(-1, LANES))
    return (
        grid_output.reshape(lat_rows, lon_cols, width),
        second.reshape(1, 1, nodes, width),
    )


def solution(mesh):
    edge = P("gx", "gy", None)
    return jax.shard_map(
        on_device,
        mesh=mesh,
        in_specs=(
            P("gx", "gy", None),
            P("gx", "gy", None, None),
            *([P()] * 6),
            *([edge] * 6),
        ),
        out_specs=(P("gx", "gy", None), P("gx", "gy", None, None)),
        check_vma=False,
    )
```

```python
import jax
import jax.numpy as jnp
from jax import lax
from jax.experimental import pallas as pl
from jax.experimental.pallas import tpu as pltpu
from jax.sharding import PartitionSpec as P

HALO = 8
LON_DEV = 64
EPSILON = 1e-05
LANES = 128
CHUNK = 256


def column(index, rows):
    parts = []
    for i in range(rows.start // LANES, rows.stop // LANES):
        row = jnp.broadcast_to(index[i : i + 1, :], (LANES, LANES))
        parts.append(row.T)
    return jnp.concatenate(parts, axis=0)


def pick(col, count):
    lane = lax.broadcasted_iota(jnp.int32, col.shape, 1)
    parts = [
        jnp.where(col == lane + k, 1.0, 0.0).astype(jnp.bfloat16)
        for k in range(0, count, LANES)
    ]
    return jnp.concatenate(parts, axis=1)


def spread(index, count):
    sub = lax.broadcasted_iota(jnp.int32, (count, LANES), 0)
    parts = [
        jnp.where(index[i : i + 1, :] == sub, 1.0, 0.0).astype(jnp.bfloat16)
        for i in range(index.shape[0])
    ]
    return jnp.concatenate(parts, axis=1)


def dot(a, b):
    return jnp.dot(a, b, preferred_element_type=jnp.float32)


def message(summed):
    half = 0.5 * summed
    return (half * jnp.tanh(half) + half).astype(jnp.bfloat16)


def refresh(latent, summed, weight):
    scaled = summed * lax.rsqrt(jnp.mean(summed * summed, axis=-1, keepdims=True) + EPSILON)
    return (latent.astype(jnp.float32) + dot(scaled.astype(jnp.bfloat16), weight)).astype(
        jnp.bfloat16
    )


def log2(value):
    assert value & (value - 1) == 0
    return value.bit_length() - 1


def edges_kernel(grid, slots, far_out, near_out, slots_out, held, sems):
    even = lax.rem(lax.axis_index("gx"), 2) == 0
    last = grid.shape[0] - 1
    near = pltpu.make_async_copy(grid.at[jnp.where(even, last, 0)], near_out, sems.at[0])
    far = pltpu.make_async_copy(grid.at[jnp.where(even, 0, last)], far_out, sems.at[1])
    index = pltpu.make_async_copy(slots, held, sems.at[2])
    index.start()
    near.start()
    far.start()
    count = held.shape[0]
    groups = slots_out.shape[0] // count
    cap = LANES // groups
    index.wait()
    for g in range(groups):
        moved = pltpu.roll(held[...], LANES - g * cap, 1) if g else held[...]
        slots_out[pl.ds(g, count, stride=groups), :] = moved
    near.wait()
    far.wait()


def sides_kernel(far, grid, near, slots, far_out, near_out, slots_out, held, sems):
    even = lax.rem(lax.axis_index("gy"), 2) == 0
    lats, lons, _ = grid.shape
    west = pltpu.make_async_copy(grid.at[:, :HALO], held.at[0], sems.at[0])
    east = pltpu.make_async_copy(grid.at[:, lons - HALO :], held.at[1], sems.at[1])
    west.start()
    east.start()
    count = slots_out.shape[0]
    groups = slots.shape[0] // count
    cap = LANES // groups
    lane = lax.broadcasted_iota(jnp.int32, slots_out.shape, 1)
    kept = jnp.zeros_like(lane)
    for g in range(groups):
        part = slots[pl.ds(g, count, stride=groups), :]
        moved = pltpu.roll(part, g * cap, 1) if g else part
        kept = jnp.where((lane >= g * cap) & (lane < (g + 1) * cap), moved, kept)
    slots_out[...] = kept
    west.wait()
    east.wait()

    def put(out, side):
        out[0] = near[side, :]
        for i in range(lats):
            out[i + 1] = held[0 if side.start == 0 else 1, i]
        out[lats + 1] = far[side, :]

    first, last = slice(0, HALO), slice(lons - HALO, lons)

    @pl.when(even)
    def _():
        put(near_out, last)
        put(far_out, first)

    @pl.when(jnp.logical_not(even))
    def _():
        put(near_out, first)
        put(far_out, last)


def places(source, lats, lons):
    band, sector = lax.axis_index("gx"), lax.axis_index("gy")
    lon_total = lons * lax.axis_size("gy")
    lat = (source >> log2(lon_total)) - band * lats + 1
    outer = (lat == 0) | (lat == lats + 1)
    lat = jnp.where(outer & (lax.rem(band, 2) == 0), lats + 1 - lat, lat)
    lon = ((source & (lon_total - 1)) - sector * lons + HALO) & (lon_total - 1)
    inner = (lon >= HALO) & (lon < HALO + lons)
    return lat, lon, inner


def gather_kernel(
    far, grid, near, mesh, w_message, w_update, w_next, source, target,
    partial, spread_out, mesh_out, w_out, held, source_held, target_held, table, sems,
):
    pairs = [(source, source_held), (target, target_held)]
    pairs += [(grid, held), (w_message, w_out.at[0]), (mesh, mesh_out)]
    pairs += [(w_update, w_out.at[1]), (w_next, w_out.at[2])]
    copies = [pltpu.make_async_copy(a, b, sems.at[i]) for i, (a, b) in enumerate(pairs)]
    for copy in copies:
        copy.start()
    lats, lons, width = grid.shape
    nodes = mesh.shape[0]
    copies[0].wait()
    copies[1].wait()
    lat, lon, inner = places(source_held[...], lats, lons)
    src = jnp.where(inner, lat * lons + lon - HALO, -1)
    tgt = target_held[...]
    edges = src.shape[0] * LANES
    spread_out[...] = spread(tgt, nodes)
    copies[2].wait()
    copies[3].wait()
    w = w_out[0]
    table[:lons, :] = dot(near[...], w).astype(jnp.bfloat16)
    inside = held[...].reshape(lats * lons, width)
    table[lons : (lats + 1) * lons, :] = dot(inside, w).astype(jnp.bfloat16)
    table[(lats + 1) * lons :, :] = dot(far[...], w).astype(jnp.bfloat16)
    copies[4].wait()
    depth = table.shape[0]
    for c in range(0, edges, CHUNK):
        rows = slice(c, c + CHUNK)
        acc = dot(pick(column(src, rows), depth), table[...])
        partial[rows, :] = acc + dot(pick(column(tgt, rows), nodes), mesh_out[...])
    copies[5].wait()
    copies[6].wait()


def encode_kernel(
    partial, other, mate, spreading, mesh, weights, source, request,
    first_out, send_out, table, messages,
):
    w = weights[0]
    tall, halo, width = mate.shape
    side = tall * halo
    table[:side, :] = dot(mate[...].reshape(side, width), w).astype(jnp.bfloat16)
    table[side : 2 * side, :] = dot(other[...].reshape(side, width), w).astype(jnp.bfloat16)
    depth = table.shape[0]
    table[2 * side :, :] = jnp.zeros((depth - 2 * side, width), jnp.bfloat16)
    nodes = mesh.shape[0]
    lons = LON_DEV
    lat, lon, inner = places(source[...], tall - 2, lons)
    on_mate = (lon >= HALO) == (lax.rem(lax.axis_index("gy"), 2) == 0)
    src = jnp.where(on_mate, 0, side) + lat * halo + (lon & (halo - 1))
    src = jnp.where(inner, -1, src)
    req = request[...]
    edges = src.shape[0] * LANES
    for c in range(0, edges, CHUNK):
        rows = slice(c, c + CHUNK)
        acc = dot(pick(column(src, rows), depth), table[...])
        messages[rows, :] = message(partial[rows, :] + acc)
    summed = dot(spreading[...], messages[...])
    first = refresh(mesh[...], summed, weights[1])
    first_out[...] = first
    following = dot(first, weights[2]).astype(jnp.bfloat16)
    for c in range(0, edges, CHUNK):
        rows = slice(c, c + CHUNK)
        send_out[rows, :] = dot(pick(column(req, rows), nodes), following).astype(jnp.bfloat16)


def process_kernel(
    picked, first, w_update, w_next, target, second_out, table_out, messages
):
    latent = first[...]
    nodes = latent.shape[0]
    tgt = target[...]
    edges = tgt.shape[0] * LANES
    for c in range(0, edges, CHUNK):
        rows = slice(c, c + CHUNK)
        acc = dot(pick(column(tgt, rows), nodes), latent)
        messages[rows, :] = message(acc + picked[rows, :].astype(jnp.float32))
    summed = dot(spread(tgt, nodes), messages[...])
    second = refresh(latent, summed, w_update[...])
    second_out[...] = second
    table_out[...] = dot(second, w_next[...]).astype(jnp.bfloat16)


def reach_kernel(own, grid, source, target, partial):
    latent = grid[...]
    cells = latent.shape[0]
    nodes = own.shape[0]
    src, tgt = source[...], target[...]
    edges = src.shape[0] * LANES
    for c in range(0, edges, CHUNK):
        rows = slice(c, c + CHUNK)
        acc = dot(pick(column(tgt, rows), cells), latent)
        partial[rows, :] = acc + dot(pick(column(src, rows), nodes), own[...])


def decode_kernel(
    partial, other, mate, grid, w_update, source, target, grid_out, messages
):
    latent = grid[...]
    cells = latent.shape[0]
    nodes = mate.shape[0]
    src, tgt = source[...], target[...]
    edges = src.shape[0] * LANES
    for c in range(0, edges, CHUNK):
        rows = slice(c, c + CHUNK)
        col = column(src, rows)
        acc = partial[rows, :]
        for at, ref in ((nodes, mate), (2 * nodes, other)):
            acc = acc + dot(pick(col - at, nodes), ref[...])
        messages[rows, :] = message(acc)
    summed = dot(spread(tgt, cells), messages[...])
    grid_out[...] = refresh(latent, summed, w_update[...])


def on_device(
    grid_latent,
    mesh_latent,
    encode_message,
    encode_update,
    process_message,
    process_update,
    decode_message,
    decode_update,
    encode_source,
    encode_target,
    process_source,
    process_target,
    decode_source,
    decode_target,
):
    lat_rows, lon_cols, width = grid_latent.shape
    bands = lax.axis_size("gx")
    sectors = lax.axis_size("gy")
    sector = lax.axis_index("gy")
    mesh_rows = mesh_latent.reshape(-1, width)
    nodes = mesh_rows.shape[0]
    grid_rows = grid_latent.reshape(-1, width)
    cells = grid_rows.shape[0]
    edges = encode_source.size
    bf16 = jnp.bfloat16
    params = pltpu.CompilerParams(vmem_limit_bytes=40 * 1024 * 1024)
    hbm = pl.BlockSpec(memory_space=pltpu.HBM)
    vmem = pl.BlockSpec(memory_space=pltpu.VMEM)
    assert lon_cols == LON_DEV

    def pinned(array):
        return pltpu.with_memory_space_constraint(array, pltpu.HBM)

    partner = [i + 1 if i % 2 else i - 1 for i in range(max(bands, sectors))]
    far_bands = [(i, partner[i]) for i in range(1, bands - 1)]
    near_bands = [(i, i ^ 1) for i in range(bands)]
    far_sectors = [(i, partner[i] % sectors) for i in range(sectors)]
    near_sectors = [(i, i ^ 1) for i in range(sectors)]

    band_edge = jax.ShapeDtypeStruct((lon_cols, width), bf16)
    far, near, slots = pl.pallas_call(
        edges_kernel,
        in_specs=[hbm, hbm],
        out_specs=(vmem,) * 3,
        out_shape=(band_edge, band_edge, jax.ShapeDtypeStruct((sectors, LANES), jnp.int32)),
        scratch_shapes=[
            pltpu.VMEM((edges // LANES, LANES), jnp.int32),
            pltpu.SemaphoreType.DMA((3,)),
        ],
        compiler_params=params,
    )(pinned(grid_latent), pinned(process_source.reshape(-1, LANES)))
    far = lax.ppermute(far, "gx", far_bands)
    near = lax.ppermute(near, "gx", near_bands)
    slots = lax.all_to_all(slots, "gy", 0, 0, tiled=True)
    sector_edge = jax.ShapeDtypeStruct((lat_rows + 2, HALO, width), bf16)
    other, mate, request = pl.pallas_call(
        sides_kernel,
        in_specs=[vmem, hbm, vmem, vmem],
        out_specs=(vmem,) * 3,
        out_shape=(
            sector_edge, sector_edge, jax.ShapeDtypeStruct((edges // LANES, LANES), jnp.int32)
        ),
        scratch_shapes=[
            pltpu.VMEM((2, lat_rows, HALO, width), bf16),
            pltpu.SemaphoreType.DMA((2,)),
        ],
        compiler_params=params,
    )(far, pinned(grid_latent), near, slots)
    other = lax.ppermute(other, "gy", far_sectors)
    mate = lax.ppermute(mate, "gy", near_sectors)

    source = encode_source.reshape(-1, LANES)
    tall_cells = (lat_rows + 2) * lon_cols
    side = (lat_rows + 2) * HALO
    partial, spreading, mesh_held, weights = pl.pallas_call(
        gather_kernel,
        in_specs=[vmem, hbm, vmem] + [hbm] * 6,
        out_specs=(vmem,) * 4,
        out_shape=(
            jax.ShapeDtypeStruct((edges, width), jnp.float32),
            jax.ShapeDtypeStruct((nodes, edges), bf16),
            jax.ShapeDtypeStruct((nodes, width), bf16),
            jax.ShapeDtypeStruct((3, width, width), bf16),
        ),
        scratch_shapes=[
            pltpu.VMEM((lat_rows, lon_cols, width), bf16),
            pltpu.VMEM((edges // LANES, LANES), jnp.int32),
            pltpu.VMEM((edges // LANES, LANES), jnp.int32),
            pltpu.VMEM((tall_cells, width), bf16),
            pltpu.SemaphoreType.DMA((7,)),
        ],
        compiler_params=params,
    )(
        far, pinned(grid_latent), near, pinned(mesh_rows), pinned(encode_message),
        pinned(encode_update), pinned(process_message),
        pinned(source), pinned(encode_target.reshape(-1, LANES)),
    )
    first, send = pl.pallas_call(
        encode_kernel,
        out_shape=(
            jax.ShapeDtypeStruct((nodes, width), bf16),
            jax.ShapeDtypeStruct((edges, width), bf16),
        ),
        scratch_shapes=[
            pltpu.VMEM((-(-2 * side // LANES) * LANES, width), bf16),
            pltpu.VMEM((edges, width), bf16),
        ],
        compiler_params=params,
    )(partial, other, mate, spreading, mesh_held, weights, source, request)
    picked = lax.all_to_all(
        send.reshape(sectors, -1, width), "gy", 0, 0, tiled=True
    ).reshape(edges, width)
    second, table = pl.pallas_call(
        process_kernel,
        out_shape=(
            jax.ShapeDtypeStruct((nodes, width), bf16),
            jax.ShapeDtypeStruct((nodes, width), bf16),
        ),
        scratch_shapes=[pltpu.VMEM((edges, width), bf16)],
        compiler_params=params,
    )(picked, first, process_update, decode_message, process_target.reshape(-1, LANES))

    other = lax.ppermute(table, "gy", far_sectors)
    mate = lax.ppermute(table, "gy", near_sectors)
    source = decode_source.reshape(-1, LANES)
    owner = source // nodes % sectors
    piece = jnp.where(owner == sector, 0, jnp.where(owner == sector ^ 1, 1, 2))
    row = piece * nodes + source % nodes
    target = decode_target.reshape(-1, LANES)
    partial = pl.pallas_call(
        reach_kernel,
        out_shape=jax.ShapeDtypeStruct((edges, width), jnp.float32),
        compiler_params=params,
    )(table, grid_rows, row, target)
    grid_output = pl.pallas_call(
        decode_kernel,
        out_shape=jax.ShapeDtypeStruct((cells, width), bf16),
        scratch_shapes=[pltpu.VMEM((edges, width), bf16)],
        compiler_params=params,
    )(partial, other, mate, grid_rows, decode_update, row, target)
    return (
        grid_output.reshape(lat_rows, lon_cols, width),
        second.reshape(1, 1, nodes, width),
    )


def solution(mesh):
    edge = P("gx", "gy", None)
    return jax.shard_map(
        on_device,
        mesh=mesh,
        in_specs=(
            P("gx", "gy", None),
            P("gx", "gy", None, None),
            *([P()] * 6),
            *([edge] * 6),
        ),
        out_specs=(P("gx", "gy", None), P("gx", "gy", None, None)),
        check_vma=False,
    )
```

```python
import functools

import jax
import jax.numpy as jnp
from jax import lax
from jax.experimental import pallas as pl
from jax.experimental.pallas import tpu as pltpu
from jax.sharding import PartitionSpec as P

HALO = 8
LON_DEV = 64
EPSILON = 1e-05
LANES = 128
CHUNK = 256
CAP = 16
GROUPS = LANES // CAP
HALF = 8


def column(index, rows):
    parts = []
    for i in range(rows.start // LANES, rows.stop // LANES):
        row = jnp.broadcast_to(index[i : i + 1, :], (LANES, LANES))
        parts.append(row.T)
    return jnp.concatenate(parts, axis=0)


def pick(col, count):
    lane = lax.broadcasted_iota(jnp.int32, col.shape, 1)
    parts = [
        jnp.where(col == lane + k, 1.0, 0.0).astype(jnp.bfloat16)
        for k in range(0, count, LANES)
    ]
    return jnp.concatenate(parts, axis=1)


def spread(index, count):
    sub = lax.broadcasted_iota(jnp.int32, (count, LANES), 0)
    parts = [
        jnp.where(index[i : i + 1, :] == sub, 1.0, 0.0).astype(jnp.bfloat16)
        for i in range(index.shape[0])
    ]
    return jnp.concatenate(parts, axis=1)


def dot(a, b):
    return jnp.dot(a, b, preferred_element_type=jnp.float32)


def message(summed):
    half = 0.5 * summed
    return (half * jnp.tanh(half) + half).astype(jnp.bfloat16)


def refresh(latent, summed, weight):
    scaled = summed * lax.rsqrt(jnp.mean(summed * summed, axis=-1, keepdims=True) + EPSILON)
    return (latent.astype(jnp.float32) + dot(scaled.astype(jnp.bfloat16), weight)).astype(
        jnp.bfloat16
    )


def log2(value):
    assert value & (value - 1) == 0
    return value.bit_length() - 1


def roll(value, shift):
    return pltpu.roll(value, shift % LANES, 1) if shift % LANES else value


def halves(index):
    upper = lax.rem(lax.axis_index("gy") // HALF, 2) == 1
    count = index.shape[0] // 2
    low = index[pl.ds(0, count, stride=2), :]
    high = index[pl.ds(1, count, stride=2), :]
    return jnp.where(upper, high, low), jnp.where(upper, low, high)


def edges_kernel(grid, slots, far_out, near_out, slots_out, held, sems):
    even = lax.rem(lax.axis_index("gx"), 2) == 0
    last = grid.shape[0] - 1
    near = pltpu.make_async_copy(grid.at[jnp.where(even, last, 0)], near_out, sems.at[0])
    far = pltpu.make_async_copy(grid.at[jnp.where(even, 0, last)], far_out, sems.at[1])
    index = pltpu.make_async_copy(slots, held, sems.at[2])
    index.start()
    near.start()
    far.start()
    index.wait()
    own, mirror = halves(held)
    lane = lax.broadcasted_iota(jnp.int32, own.shape, 1)
    for g in range(GROUPS):
        first = roll(own, -g * CAP)
        second = roll(mirror, CAP - g * CAP)
        slots_out[pl.ds(g, own.shape[0], stride=GROUPS), :] = jnp.where(lane < CAP, first, second)
    near.wait()
    far.wait()


def sides_kernel(far, grid, near, slots, far_out, near_out, slots_out, held, sems):
    even = lax.rem(lax.axis_index("gy"), 2) == 0
    lats, lons, _ = grid.shape
    west = pltpu.make_async_copy(grid.at[:, :HALO], held.at[0], sems.at[0])
    east = pltpu.make_async_copy(grid.at[:, lons - HALO :], held.at[1], sems.at[1])
    west.start()
    east.start()
    count = slots_out.shape[0] // 2
    lane = lax.broadcasted_iota(jnp.int32, (count, LANES), 1)
    for half in range(2):
        kept = jnp.zeros_like(lane)
        for g in range(GROUPS):
            part = slots[pl.ds(g, count, stride=GROUPS), :]
            moved = roll(part, g * CAP - half * CAP)
            kept = jnp.where((lane >= g * CAP) & (lane < (g + 1) * CAP), moved, kept)
        slots_out[half * count : (half + 1) * count, :] = kept
    west.wait()
    east.wait()

    def put(out, side):
        out[0] = near[side, :]
        for i in range(lats):
            out[i + 1] = held[0 if side.start == 0 else 1, i]
        out[lats + 1] = far[side, :]

    first, last = slice(0, HALO), slice(lons - HALO, lons)

    @pl.when(even)
    def _():
        put(near_out, last)
        put(far_out, first)

    @pl.when(jnp.logical_not(even))
    def _():
        put(near_out, first)
        put(far_out, last)


def places(source, lats, lons):
    band, sector = lax.axis_index("gx"), lax.axis_index("gy")
    lon_total = lons * lax.axis_size("gy")
    lat = (source >> log2(lon_total)) - band * lats + 1
    outer = (lat == 0) | (lat == lats + 1)
    lat = jnp.where(outer & (lax.rem(band, 2) == 0), lats + 1 - lat, lat)
    lon = ((source & (lon_total - 1)) - sector * lons + HALO) & (lon_total - 1)
    inner = (lon >= HALO) & (lon < HALO + lons)
    return lat, lon, inner


def gather_kernel(
    far, grid, near, mesh, w_message, w_update, w_next, source, target,
    partial, spread_out, mesh_out, w_out, held, source_held, target_held, table, sems,
):
    pairs = [(source, source_held), (target, target_held)]
    pairs += [(grid, held), (w_message, w_out.at[0]), (mesh, mesh_out)]
    pairs += [(w_update, w_out.at[1]), (w_next, w_out.at[2])]
    copies = [pltpu.make_async_copy(a, b, sems.at[i]) for i, (a, b) in enumerate(pairs)]
    for copy in copies:
        copy.start()
    lats, lons, width = grid.shape
    nodes = mesh.shape[0]
    copies[0].wait()
    copies[1].wait()
    lat, lon, inner = places(source_held[...], lats, lons)
    src = jnp.where(inner, lat * lons + lon - HALO, -1)
    tgt = target_held[...]
    edges = src.shape[0] * LANES
    spread_out[...] = spread(tgt, nodes)
    copies[2].wait()
    copies[3].wait()
    w = w_out[0]
    table[:lons, :] = dot(near[...], w).astype(jnp.bfloat16)
    inside = held[...].reshape(lats * lons, width)
    table[lons : (lats + 1) * lons, :] = dot(inside, w).astype(jnp.bfloat16)
    table[(lats + 1) * lons :, :] = dot(far[...], w).astype(jnp.bfloat16)
    copies[4].wait()
    depth = table.shape[0]
    for c in range(0, edges, CHUNK):
        rows = slice(c, c + CHUNK)
        acc = dot(pick(column(src, rows), depth), table[...])
        partial[rows, :] = acc + dot(pick(column(tgt, rows), nodes), mesh_out[...])
    copies[5].wait()
    copies[6].wait()


def encode_kernel(
    partial, other, mate, spreading, mesh, weights, source,
    first_out, next_out, table, messages,
):
    w = weights[0]
    tall, halo, width = mate.shape
    side = tall * halo
    table[:side, :] = dot(mate[...].reshape(side, width), w).astype(jnp.bfloat16)
    table[side : 2 * side, :] = dot(other[...].reshape(side, width), w).astype(jnp.bfloat16)
    depth = table.shape[0]
    table[2 * side :, :] = jnp.zeros((depth - 2 * side, width), jnp.bfloat16)
    nodes = mesh.shape[0]
    lons = LON_DEV
    lat, lon, inner = places(source[...], tall - 2, lons)
    on_mate = (lon >= HALO) == (lax.rem(lax.axis_index("gy"), 2) == 0)
    src = jnp.where(on_mate, 0, side) + lat * halo + (lon & (halo - 1))
    src = jnp.where(inner, -1, src)
    edges = src.shape[0] * LANES
    for c in range(0, edges, CHUNK):
        rows = slice(c, c + CHUNK)
        acc = dot(pick(column(src, rows), depth), table[...])
        messages[rows, :] = message(partial[rows, :] + acc)
    summed = dot(spreading[...], messages[...])
    first = refresh(mesh[...], summed, weights[1])
    first_out[...] = first
    next_out[...] = dot(first, weights[2]).astype(jnp.bfloat16)


def request_kernel(half, table, request, send_out):
    nodes = table.shape[0]
    count = request.shape[0] // 2
    req = request[half * count : (half + 1) * count, :]
    for c in range(0, count * LANES, CHUNK):
        rows = slice(c, c + CHUNK)
        send_out[rows, :] = dot(pick(column(req, rows), nodes), table[...]).astype(jnp.bfloat16)


def half_kernel(picked, first, target, summed_out, messages):
    own, _ = halves(target)
    summed_out[...] = half_sum(picked, first[...], own, messages)


def half_sum(picked, latent, target, messages):
    nodes = latent.shape[0]
    edges = target.shape[0] * LANES
    for c in range(0, edges, CHUNK):
        rows = slice(c, c + CHUNK)
        acc = dot(pick(column(target, rows), nodes), latent)
        messages[rows, :] = message(acc + picked[rows, :].astype(jnp.float32))
    return dot(spread(target, nodes), messages[...])


def process_kernel(
    partial, picked, first, w_update, w_next, target, second_out, table_out, messages
):
    latent = first[...]
    _, mirror = halves(target)
    summed = partial[...] + half_sum(picked, latent, mirror, messages)
    second = refresh(latent, summed, w_update[...])
    second_out[...] = second
    table_out[...] = dot(second, w_next[...]).astype(jnp.bfloat16)


def reach_kernel(own, grid, source, target, partial):
    latent = grid[...]
    cells = latent.shape[0]
    nodes = own.shape[0]
    src, tgt = source[...], target[...]
    edges = src.shape[0] * LANES
    for c in range(0, edges, CHUNK):
        rows = slice(c, c + CHUNK)
        acc = dot(pick(column(tgt, rows), cells), latent)
        partial[rows, :] = acc + dot(pick(column(src, rows), nodes), own[...])


def decode_kernel(
    partial, other, mate, grid, w_update, source, target, grid_out, messages
):
    latent = grid[...]
    cells = latent.shape[0]
    nodes = mate.shape[0]
    src, tgt = source[...], target[...]
    edges = src.shape[0] * LANES
    for c in range(0, edges, CHUNK):
        rows = slice(c, c + CHUNK)
        col = column(src, rows)
        acc = partial[rows, :]
        for at, ref in ((nodes, mate), (2 * nodes, other)):
            acc = acc + dot(pick(col - at, nodes), ref[...])
        messages[rows, :] = message(acc)
    summed = dot(spread(tgt, cells), messages[...])
    grid_out[...] = refresh(latent, summed, w_update[...])


def on_device(
    grid_latent,
    mesh_latent,
    encode_message,
    encode_update,
    process_message,
    process_update,
    decode_message,
    decode_update,
    encode_source,
    encode_target,
    process_source,
    process_target,
    decode_source,
    decode_target,
):
    lat_rows, lon_cols, width = grid_latent.shape
    bands = lax.axis_size("gx")
    sectors = lax.axis_size("gy")
    sector = lax.axis_index("gy")
    mesh_rows = mesh_latent.reshape(-1, width)
    nodes = mesh_rows.shape[0]
    grid_rows = grid_latent.reshape(-1, width)
    cells = grid_rows.shape[0]
    edges = encode_source.size
    bf16 = jnp.bfloat16
    params = pltpu.CompilerParams(vmem_limit_bytes=40 * 1024 * 1024)
    hbm = pl.BlockSpec(memory_space=pltpu.HBM)
    vmem = pl.BlockSpec(memory_space=pltpu.VMEM)
    assert lon_cols == LON_DEV

    def pinned(array):
        return pltpu.with_memory_space_constraint(array, pltpu.HBM)

    partner = [i + 1 if i % 2 else i - 1 for i in range(max(bands, sectors))]
    far_bands = [(i, partner[i]) for i in range(1, bands - 1)]
    near_bands = [(i, i ^ 1) for i in range(bands)]
    far_sectors = [(i, partner[i] % sectors) for i in range(sectors)]
    near_sectors = [(i, i ^ 1) for i in range(sectors)]

    group = [[i for i in range(sectors) if i // HALF % 2 == h] for h in range(2)]

    def exchange(array):
        return lax.all_to_all(array, "gy", 0, 0, axis_index_groups=group, tiled=True)

    band_edge = jax.ShapeDtypeStruct((lon_cols, width), bf16)
    far, near, slots = pl.pallas_call(
        edges_kernel,
        in_specs=[hbm, hbm],
        out_specs=(vmem,) * 3,
        out_shape=(band_edge, band_edge, jax.ShapeDtypeStruct((sectors // 2, LANES), jnp.int32)),
        scratch_shapes=[
            pltpu.VMEM((edges // LANES, LANES), jnp.int32),
            pltpu.SemaphoreType.DMA((3,)),
        ],
        compiler_params=params,
    )(pinned(grid_latent), pinned(process_source.reshape(-1, LANES)))
    far = lax.ppermute(far, "gx", far_bands)
    near = lax.ppermute(near, "gx", near_bands)
    slots = exchange(slots)
    sector_edge = jax.ShapeDtypeStruct((lat_rows + 2, HALO, width), bf16)
    other, mate, request = pl.pallas_call(
        sides_kernel,
        in_specs=[vmem, hbm, vmem, vmem],
        out_specs=(vmem,) * 3,
        out_shape=(
            sector_edge, sector_edge, jax.ShapeDtypeStruct((edges // LANES, LANES), jnp.int32)
        ),
        scratch_shapes=[
            pltpu.VMEM((2, lat_rows, HALO, width), bf16),
            pltpu.SemaphoreType.DMA((2,)),
        ],
        compiler_params=params,
    )(far, pinned(grid_latent), near, slots)
    other = lax.ppermute(other, "gy", far_sectors)
    mate = lax.ppermute(mate, "gy", near_sectors)

    source = encode_source.reshape(-1, LANES)
    tall_cells = (lat_rows + 2) * lon_cols
    side = (lat_rows + 2) * HALO
    partial, spreading, mesh_held, weights = pl.pallas_call(
        gather_kernel,
        in_specs=[vmem, hbm, vmem] + [hbm] * 6,
        out_specs=(vmem,) * 4,
        out_shape=(
            jax.ShapeDtypeStruct((edges, width), jnp.float32),
            jax.ShapeDtypeStruct((nodes, edges), bf16),
            jax.ShapeDtypeStruct((nodes, width), bf16),
            jax.ShapeDtypeStruct((3, width, width), bf16),
        ),
        scratch_shapes=[
            pltpu.VMEM((lat_rows, lon_cols, width), bf16),
            pltpu.VMEM((edges // LANES, LANES), jnp.int32),
            pltpu.VMEM((edges // LANES, LANES), jnp.int32),
            pltpu.VMEM((tall_cells, width), bf16),
            pltpu.SemaphoreType.DMA((7,)),
        ],
        compiler_params=params,
    )(
        far, pinned(grid_latent), near, pinned(mesh_rows), pinned(encode_message),
        pinned(encode_update), pinned(process_message),
        pinned(source), pinned(encode_target.reshape(-1, LANES)),
    )
    first, following = pl.pallas_call(
        encode_kernel,
        out_shape=(
            jax.ShapeDtypeStruct((nodes, width), bf16),
            jax.ShapeDtypeStruct((nodes, width), bf16),
        ),
        scratch_shapes=[
            pltpu.VMEM((-(-2 * side // LANES) * LANES, width), bf16),
            pltpu.VMEM((edges, width), bf16),
        ],
        compiler_params=params,
    )(partial, other, mate, spreading, mesh_held, weights, source)

    def requested(half, table):
        rows = pl.pallas_call(
            functools.partial(request_kernel, half),
            out_shape=jax.ShapeDtypeStruct((edges // 2, width), bf16),
            compiler_params=params,
            cost_estimate=pl.CostEstimate(
                flops=half * 35 * 10**9, bytes_accessed=10**6, transcendentals=0
            ),
        )(table, request)
        return exchange(rows.reshape(sectors // 2, -1, width)).reshape(edges // 2, width)

    mirror = lax.ppermute(following, "gy", [(i, i ^ HALF) for i in range(sectors)])
    target = process_target.reshape(-1, LANES)
    messages = pltpu.VMEM((edges // 2, width), bf16)
    partial = pl.pallas_call(
        half_kernel,
        out_shape=jax.ShapeDtypeStruct((nodes, width), jnp.float32),
        scratch_shapes=[messages],
        compiler_params=params,
    )(requested(0, following), first, target)
    second, table = pl.pallas_call(
        process_kernel,
        out_shape=(
            jax.ShapeDtypeStruct((nodes, width), bf16),
            jax.ShapeDtypeStruct((nodes, width), bf16),
        ),
        scratch_shapes=[messages],
        compiler_params=params,
    )(partial, requested(1, mirror), first, process_update, decode_message, target)

    other = lax.ppermute(table, "gy", far_sectors)
    mate = lax.ppermute(table, "gy", near_sectors)
    source = decode_source.reshape(-1, LANES)
    owner = source // nodes % sectors
    piece = jnp.where(owner == sector, 0, jnp.where(owner == sector ^ 1, 1, 2))
    row = piece * nodes + source % nodes
    target = decode_target.reshape(-1, LANES)
    partial = pl.pallas_call(
        reach_kernel,
        out_shape=jax.ShapeDtypeStruct((edges, width), jnp.float32),
        compiler_params=params,
    )(table, grid_rows, row, target)
    grid_output = pl.pallas_call(
        decode_kernel,
        out_shape=jax.ShapeDtypeStruct((cells, width), bf16),
        scratch_shapes=[pltpu.VMEM((edges, width), bf16)],
        compiler_params=params,
    )(partial, other, mate, grid_rows, decode_update, row, target)
    return (
        grid_output.reshape(lat_rows, lon_cols, width),
        second.reshape(1, 1, nodes, width),
    )


def solution(mesh):
    edge = P("gx", "gy", None)
    return jax.shard_map(
        on_device,
        mesh=mesh,
        in_specs=(
            P("gx", "gy", None),
            P("gx", "gy", None, None),
            *([P()] * 6),
            *([edge] * 6),
        ),
        out_specs=(P("gx", "gy", None), P("gx", "gy", None, None)),
        check_vma=False,
    )
```

```python
import jax
import jax.numpy as jnp
from jax import lax
from jax.experimental import pallas as pl
from jax.experimental.pallas import tpu as pltpu
from jax.sharding import PartitionSpec as P

HALO = 8
LON_DEV = 64
EPSILON = 1e-05
LANES = 128
CHUNK = 256
CAP = 16
GROUPS = LANES // CAP
HALF = 8


def column(index, rows):
    parts = []
    for i in range(rows.start // LANES, rows.stop // LANES):
        row = jnp.broadcast_to(index[i : i + 1, :], (LANES, LANES))
        parts.append(row.T)
    return jnp.concatenate(parts, axis=0)


def pick(col, count):
    lane = lax.broadcasted_iota(jnp.int32, col.shape, 1)
    parts = [
        jnp.where(col == lane + k, 1.0, 0.0).astype(jnp.bfloat16)
        for k in range(0, count, LANES)
    ]
    return jnp.concatenate(parts, axis=1)


def spread(index, count):
    sub = lax.broadcasted_iota(jnp.int32, (count, LANES), 0)
    parts = [
        jnp.where(index[i : i + 1, :] == sub, 1.0, 0.0).astype(jnp.bfloat16)
        for i in range(index.shape[0])
    ]
    return jnp.concatenate(parts, axis=1)


def dot(a, b):
    return jnp.dot(a, b, preferred_element_type=jnp.float32)


def message(summed):
    half = 0.5 * summed
    return (half * jnp.tanh(half) + half).astype(jnp.bfloat16)


def refresh(latent, summed, weight):
    scaled = summed * lax.rsqrt(jnp.mean(summed * summed, axis=-1, keepdims=True) + EPSILON)
    return (latent.astype(jnp.float32) + dot(scaled.astype(jnp.bfloat16), weight)).astype(
        jnp.bfloat16
    )


def log2(value):
    assert value & (value - 1) == 0
    return value.bit_length() - 1


def roll(value, shift):
    return pltpu.roll(value, shift % LANES, 1) if shift % LANES else value


def halves(index):
    upper = lax.rem(lax.axis_index("gy") // HALF, 2) == 1
    count = index.shape[0] // 2
    low = index[pl.ds(0, count, stride=2), :]
    high = index[pl.ds(1, count, stride=2), :]
    return jnp.where(upper, high, low), jnp.where(upper, low, high)


def apart(slots, out):
    own, mirror = halves(slots)
    lane = lax.broadcasted_iota(jnp.int32, own.shape, 1)
    for g in range(GROUPS):
        first = roll(own, -g * CAP)
        second = roll(mirror, CAP - g * CAP)
        out[pl.ds(g, own.shape[0], stride=GROUPS), :] = jnp.where(lane < CAP, first, second)


def together(rows):
    each = 2 * CAP
    fold = LANES // each
    count = rows.shape[0] // fold
    lane = lax.broadcasted_iota(jnp.int32, (count, LANES), 1)
    kept = jnp.zeros_like(lane)
    for g in range(fold):
        moved = roll(rows[pl.ds(g, count, stride=fold), :], g * each)
        kept = jnp.where((lane >= g * each) & (lane < (g + 1) * each), moved, kept)
    return kept


def edges_kernel(grid, far_out, near_out, sems):
    even = lax.rem(lax.axis_index("gx"), 2) == 0
    last = grid.shape[0] - 1
    near = pltpu.make_async_copy(grid.at[jnp.where(even, last, 0)], near_out, sems.at[0])
    far = pltpu.make_async_copy(grid.at[jnp.where(even, 0, last)], far_out, sems.at[1])
    near.start()
    far.start()
    near.wait()
    far.wait()


def sides_kernel(far, grid, near, far_out, near_out, held, sems):
    even = lax.rem(lax.axis_index("gy"), 2) == 0
    lats, lons, _ = grid.shape
    west = pltpu.make_async_copy(grid.at[:, :HALO], held.at[0], sems.at[0])
    east = pltpu.make_async_copy(grid.at[:, lons - HALO :], held.at[1], sems.at[1])
    west.start()
    east.start()
    west.wait()
    east.wait()

    def put(out, side):
        out[0] = near[side, :]
        for i in range(lats):
            out[i + 1] = held[0 if side.start == 0 else 1, i]
        out[lats + 1] = far[side, :]

    first, last = slice(0, HALO), slice(lons - HALO, lons)

    @pl.when(even)
    def _():
        put(near_out, last)
        put(far_out, first)

    @pl.when(jnp.logical_not(even))
    def _():
        put(near_out, first)
        put(far_out, last)


def places(source, lats, lons):
    band, sector = lax.axis_index("gx"), lax.axis_index("gy")
    lon_total = lons * lax.axis_size("gy")
    lat = (source >> log2(lon_total)) - band * lats + 1
    outer = (lat == 0) | (lat == lats + 1)
    lat = jnp.where(outer & (lax.rem(band, 2) == 0), lats + 1 - lat, lat)
    lon = ((source & (lon_total - 1)) - sector * lons + HALO) & (lon_total - 1)
    inner = (lon >= HALO) & (lon < HALO + lons)
    return lat, lon, inner


def gather_kernel(
    far, grid, near, mesh, w_message, w_update, w_next, source, target, next_source, next_target,
    partial, spread_out, mesh_out, w_out, sides_out, slots_out, order_out,
    held, indices, rows_held, table, sems,
):
    pairs = [(source, indices.at[0]), (target, indices.at[1])]
    pairs += [(grid, held), (w_message, w_out.at[0]), (mesh, mesh_out)]
    pairs += [(next_source, indices.at[2]), (next_target, indices.at[3])]
    pairs += [(w_update, w_out.at[1]), (w_next, w_out.at[2])]
    copies = [pltpu.make_async_copy(a, b, sems.at[i]) for i, (a, b) in enumerate(pairs)]
    for copy in copies:
        copy.start()
    lats, lons, width = grid.shape
    nodes = mesh.shape[0]
    copies[0].wait()
    copies[1].wait()
    lat, lon, inner = places(indices[0], lats, lons)
    src = jnp.where(inner, lat * lons + lon - HALO, -1)
    tgt = indices[1]
    edges = src.shape[0] * LANES
    spread_out[...] = spread(tgt, nodes)
    copies[2].wait()
    copies[3].wait()
    w = w_out[0]
    table[:lons, :] = dot(near[...], w).astype(jnp.bfloat16)
    inside = held[...].reshape(lats * lons, width)
    table[lons : (lats + 1) * lons, :] = dot(inside, w).astype(jnp.bfloat16)
    table[(lats + 1) * lons :, :] = dot(far[...], w).astype(jnp.bfloat16)
    copies[4].wait()
    depth = table.shape[0]
    side = (lats + 2) * HALO
    on_mate = (lon >= HALO) == (lax.rem(lax.axis_index("gy"), 2) == 0)
    edge = jnp.where(on_mate, 0, side) + lat * HALO + (lon & (HALO - 1))
    edge = jnp.where(inner, -1, edge)
    for c in range(0, edges, CHUNK):
        rows = slice(c, c + CHUNK)
        acc = dot(pick(column(src, rows), depth), table[...])
        partial[rows, :] = acc + dot(pick(column(tgt, rows), nodes), mesh_out[...])
        sides_out[rows, :] = pick(column(edge, rows), sides_out.shape[1])
    copies[5].wait()
    copies[6].wait()
    apart(indices.at[2], slots_out)
    apart(indices.at[3], rows_held)
    order_out[...] = together(rows_held)
    copies[7].wait()
    copies[8].wait()


def encode_kernel(
    partial, other, mate, spreading, mesh, weights, sides,
    first_out, next_out, table, messages,
):
    w = weights[0]
    tall, halo, width = mate.shape
    side = tall * halo
    table[:side, :] = dot(mate[...].reshape(side, width), w).astype(jnp.bfloat16)
    table[side : 2 * side, :] = dot(other[...].reshape(side, width), w).astype(jnp.bfloat16)
    table[2 * side :, :] = jnp.zeros((table.shape[0] - 2 * side, width), jnp.bfloat16)
    edges = partial.shape[0]
    for c in range(0, edges, CHUNK):
        rows = slice(c, c + CHUNK)
        messages[rows, :] = message(partial[rows, :] + dot(sides[rows, :], table[...]))
    summed = dot(spreading[...], messages[...])
    first = refresh(mesh[...], summed, weights[1])
    first_out[...] = first
    next_out[...] = dot(first, weights[2]).astype(jnp.bfloat16)


def request_kernel(table, mirror, slots, send_out):
    nodes = table.shape[0]
    asked = together(slots)
    lane = lax.broadcasted_iota(jnp.int32, asked.shape, 1)
    second = (lane & (2 * CAP - 1)) >= CAP
    for ref, req in ((table, jnp.where(second, -1, asked)), (mirror, jnp.where(second, asked, -1))):
        for c in range(0, send_out.shape[0], CHUNK):
            rows = slice(c, c + CHUNK)
            part = dot(pick(column(req, rows), nodes), ref[...]).astype(jnp.bfloat16)
            send_out[rows, :] = part if ref is table else send_out[rows, :] + part


def target_kernel(first, target, partial, spread_out):
    nodes = first.shape[0]
    tgt = target[...]
    for c in range(0, partial.shape[0], CHUNK):
        rows = slice(c, c + CHUNK)
        partial[rows, :] = dot(pick(column(tgt, rows), nodes), first[...])
    spread_out[...] = spread(tgt, nodes)


def process_kernel(
    picked, partial, spreading, first, w_update, w_next, second_out, table_out, messages
):
    for c in range(0, picked.shape[0], CHUNK):
        rows = slice(c, c + CHUNK)
        messages[rows, :] = message(partial[rows, :] + picked[rows, :].astype(jnp.float32))
    second = refresh(first[...], dot(spreading[...], messages[...]), w_update[...])
    second_out[...] = second
    table_out[...] = dot(second, w_next[...]).astype(jnp.bfloat16)


def reach_kernel(own, grid, source, target, partial, picks_out, spread_out):
    latent = grid[...]
    cells = latent.shape[0]
    nodes = own.shape[0]
    src, tgt = source[...], target[...]
    for c in range(0, partial.shape[0], CHUNK):
        rows = slice(c, c + CHUNK)
        col = column(src, rows)
        acc = dot(pick(column(tgt, rows), cells), latent)
        partial[rows, :] = acc + dot(pick(col, nodes), own[...])
        picks_out[rows, :] = pick(col - nodes, 2 * nodes)
    spread_out[...] = spread(tgt, cells)


def decode_kernel(
    partial, other, mate, picks, spreading, grid, w_update, grid_out, messages
):
    nodes = mate.shape[0]
    for c in range(0, partial.shape[0], CHUNK):
        rows = slice(c, c + CHUNK)
        acc = partial[rows, :] + dot(picks[rows, :nodes], mate[...])
        messages[rows, :] = message(acc + dot(picks[rows, nodes:], other[...]))
    summed = dot(spreading[...], messages[...])
    grid_out[...] = refresh(grid[...], summed, w_update[...])


def on_device(
    grid_latent,
    mesh_latent,
    encode_message,
    encode_update,
    process_message,
    process_update,
    decode_message,
    decode_update,
    encode_source,
    encode_target,
    process_source,
    process_target,
    decode_source,
    decode_target,
):
    lat_rows, lon_cols, width = grid_latent.shape
    bands = lax.axis_size("gx")
    sectors = lax.axis_size("gy")
    sector = lax.axis_index("gy")
    mesh_rows = mesh_latent.reshape(-1, width)
    nodes = mesh_rows.shape[0]
    grid_rows = grid_latent.reshape(-1, width)
    cells = grid_rows.shape[0]
    edges = encode_source.size
    bf16 = jnp.bfloat16
    params = pltpu.CompilerParams(vmem_limit_bytes=40 * 1024 * 1024)
    hbm = pl.BlockSpec(memory_space=pltpu.HBM)
    vmem = pl.BlockSpec(memory_space=pltpu.VMEM)
    assert lon_cols == LON_DEV

    def pinned(array):
        return pltpu.with_memory_space_constraint(array, pltpu.HBM)

    partner = [i + 1 if i % 2 else i - 1 for i in range(max(bands, sectors))]
    far_bands = [(i, partner[i]) for i in range(1, bands - 1)]
    near_bands = [(i, i ^ 1) for i in range(bands)]
    far_sectors = [(i, partner[i] % sectors) for i in range(sectors)]
    near_sectors = [(i, i ^ 1) for i in range(sectors)]

    group = [[i for i in range(sectors) if i // HALF % 2 == h] for h in range(2)]

    def exchange(array):
        return lax.all_to_all(array, "gy", 0, 0, axis_index_groups=group, tiled=True)

    band_edge = jax.ShapeDtypeStruct((lon_cols, width), bf16)
    far, near = pl.pallas_call(
        edges_kernel,
        in_specs=[hbm],
        out_specs=(vmem,) * 2,
        out_shape=(band_edge,) * 2,
        scratch_shapes=[pltpu.SemaphoreType.DMA((2,))],
        compiler_params=params,
    )(pinned(grid_latent))
    far = lax.ppermute(far, "gx", far_bands)
    near = lax.ppermute(near, "gx", near_bands)
    sector_edge = jax.ShapeDtypeStruct((lat_rows + 2, HALO, width), bf16)
    other, mate = pl.pallas_call(
        sides_kernel,
        in_specs=[vmem, hbm, vmem],
        out_specs=(vmem,) * 2,
        out_shape=(sector_edge,) * 2,
        scratch_shapes=[
            pltpu.VMEM((2, lat_rows, HALO, width), bf16),
            pltpu.SemaphoreType.DMA((2,)),
        ],
        compiler_params=params,
    )(far, pinned(grid_latent), near)
    other = lax.ppermute(other, "gy", far_sectors)
    mate = lax.ppermute(mate, "gy", near_sectors)

    tall_cells = (lat_rows + 2) * lon_cols
    depth = -(-2 * (lat_rows + 2) * HALO // LANES) * LANES
    index = jax.ShapeDtypeStruct((edges // LANES, LANES), jnp.int32)
    table_shape = jax.ShapeDtypeStruct((nodes, width), bf16)
    partial_shape = jax.ShapeDtypeStruct((edges, width), jnp.float32)
    spread_shape = jax.ShapeDtypeStruct((nodes, edges), bf16)
    slots_shape = jax.ShapeDtypeStruct((sectors // 2, LANES), jnp.int32)
    partial, spreading, mesh_held, weights, sides, slots, order = pl.pallas_call(
        gather_kernel,
        in_specs=[vmem, hbm, vmem] + [hbm] * 8,
        out_specs=(vmem,) * 7,
        out_shape=(
            partial_shape,
            spread_shape,
            table_shape,
            jax.ShapeDtypeStruct((3, width, width), bf16),
            jax.ShapeDtypeStruct((edges, depth), bf16),
            slots_shape,
            index,
        ),
        scratch_shapes=[
            pltpu.VMEM((lat_rows, lon_cols, width), bf16),
            pltpu.VMEM((4, edges // LANES, LANES), jnp.int32),
            pltpu.VMEM(slots_shape.shape, jnp.int32),
            pltpu.VMEM((tall_cells, width), bf16),
            pltpu.SemaphoreType.DMA((9,)),
        ],
        compiler_params=params,
    )(
        far, pinned(grid_latent), near, pinned(mesh_rows), pinned(encode_message),
        pinned(encode_update), pinned(process_message),
        *(
            pinned(array.reshape(-1, LANES))
            for array in (encode_source, encode_target, process_source, process_target)
        ),
    )
    messages = pltpu.VMEM((edges, width), bf16)
    first, following = pl.pallas_call(
        encode_kernel,
        out_shape=(table_shape, table_shape),
        scratch_shapes=[pltpu.VMEM((depth, width), bf16), messages],
        compiler_params=params,
    )(partial, other, mate, spreading, mesh_held, weights, sides)

    following, slots = lax.optimization_barrier((following, slots))
    mirror = lax.ppermute(following, "gy", [(i, i ^ HALF) for i in range(sectors)])
    slots = exchange(slots)
    partial, spreading = pl.pallas_call(
        target_kernel,
        out_shape=(partial_shape, spread_shape),
        compiler_params=params,
    )(first, order)
    send = pl.pallas_call(
        request_kernel,
        out_shape=jax.ShapeDtypeStruct((edges, width), bf16),
        compiler_params=params,
    )(following, mirror, slots)
    picked = exchange(send.reshape(sectors // 2, -1, width)).reshape(edges, width)
    second, table = pl.pallas_call(
        process_kernel,
        out_shape=(table_shape, table_shape),
        scratch_shapes=[messages],
        compiler_params=params,
    )(picked, partial, spreading, first, process_update, decode_message)

    other = lax.ppermute(table, "gy", far_sectors)
    mate = lax.ppermute(table, "gy", near_sectors)
    source = decode_source.reshape(-1, LANES)
    owner = source // nodes % sectors
    piece = jnp.where(owner == sector, 0, jnp.where(owner == sector ^ 1, 1, 2))
    row = piece * nodes + source % nodes
    target = decode_target.reshape(-1, LANES)
    partial, picks, spreading = pl.pallas_call(
        reach_kernel,
        out_shape=(
            partial_shape,
            jax.ShapeDtypeStruct((edges, 2 * nodes), bf16),
            jax.ShapeDtypeStruct((cells, edges), bf16),
        ),
        compiler_params=params,
    )(table, grid_rows, row, target)
    grid_output = pl.pallas_call(
        decode_kernel,
        out_shape=jax.ShapeDtypeStruct((cells, width), bf16),
        scratch_shapes=[messages],
        compiler_params=params,
    )(partial, other, mate, picks, spreading, grid_rows, decode_update)
    return (
        grid_output.reshape(lat_rows, lon_cols, width),
        second.reshape(1, 1, nodes, width),
    )


def solution(mesh):
    edge = P("gx", "gy", None)
    return jax.shard_map(
        on_device,
        mesh=mesh,
        in_specs=(
            P("gx", "gy", None),
            P("gx", "gy", None, None),
            *([P()] * 6),
            *([edge] * 6),
        ),
        out_specs=(P("gx", "gy", None), P("gx", "gy", None, None)),
        check_vma=False,
    )
```

```python
import jax
import jax.numpy as jnp
from jax import lax
from jax.experimental import pallas as pl
from jax.experimental.pallas import tpu as pltpu
from jax.sharding import PartitionSpec as P

HALO = 8
LON_DEV = 64
EPSILON = 1e-05
LANES = 128
CHUNK = 256
CAP = 16
GROUPS = LANES // CAP
HALF = 8


def column(index, rows):
    parts = []
    for i in range(rows.start // LANES, rows.stop // LANES):
        row = jnp.broadcast_to(index[i : i + 1, :], (LANES, LANES))
        parts.append(row.T)
    return jnp.concatenate(parts, axis=0)


def pick(col, count):
    lane = lax.broadcasted_iota(jnp.int32, col.shape, 1)
    parts = [
        jnp.where(col == lane + k, 1.0, 0.0).astype(jnp.bfloat16)
        for k in range(0, count, LANES)
    ]
    return jnp.concatenate(parts, axis=1)


def spread(index, count):
    sub = lax.broadcasted_iota(jnp.int32, (count, LANES), 0)
    parts = [
        jnp.where(index[i : i + 1, :] == sub, 1.0, 0.0).astype(jnp.bfloat16)
        for i in range(index.shape[0])
    ]
    return jnp.concatenate(parts, axis=1)


def dot(a, b):
    return jnp.dot(a, b, preferred_element_type=jnp.float32)


def message(summed):
    half = 0.5 * summed
    return (half * jnp.tanh(half) + half).astype(jnp.bfloat16)


def refresh(latent, summed, weight):
    scaled = summed * lax.rsqrt(jnp.mean(summed * summed, axis=-1, keepdims=True) + EPSILON)
    return (latent.astype(jnp.float32) + dot(scaled.astype(jnp.bfloat16), weight)).astype(
        jnp.bfloat16
    )


def log2(value):
    assert value & (value - 1) == 0
    return value.bit_length() - 1


def roll(value, shift):
    return pltpu.roll(value, shift % LANES, 1) if shift % LANES else value


def halves(index):
    upper = lax.rem(lax.axis_index("gy") // HALF, 2) == 1
    count = index.shape[0] // 2
    low = index[pl.ds(0, count, stride=2), :]
    high = index[pl.ds(1, count, stride=2), :]
    return jnp.where(upper, high, low), jnp.where(upper, low, high)


def apart(slots, out):
    own, mirror = halves(slots)
    lane = lax.broadcasted_iota(jnp.int32, own.shape, 1)
    for g in range(GROUPS):
        first = roll(own, -g * CAP)
        second = roll(mirror, CAP - g * CAP)
        out[pl.ds(g, own.shape[0], stride=GROUPS), :] = jnp.where(lane < CAP, first, second)


def together(rows):
    each = 2 * CAP
    fold = LANES // each
    count = rows.shape[0] // fold
    lane = lax.broadcasted_iota(jnp.int32, (count, LANES), 1)
    kept = jnp.zeros_like(lane)
    for g in range(fold):
        moved = roll(rows[pl.ds(g, count, stride=fold), :], g * each)
        kept = jnp.where((lane >= g * each) & (lane < (g + 1) * each), moved, kept)
    return kept


def edges_kernel(grid, far_out, near_out, sems):
    even = lax.rem(lax.axis_index("gx"), 2) == 0
    last = grid.shape[0] - 1
    near = pltpu.make_async_copy(grid.at[jnp.where(even, last, 0)], near_out, sems.at[0])
    far = pltpu.make_async_copy(grid.at[jnp.where(even, 0, last)], far_out, sems.at[1])
    near.start()
    far.start()
    near.wait()
    far.wait()


def sides_kernel(far, grid, near, far_out, near_out, held, sems):
    even = lax.rem(lax.axis_index("gy"), 2) == 0
    lats, lons, _ = grid.shape
    west = pltpu.make_async_copy(grid.at[:, :HALO], held.at[0], sems.at[0])
    east = pltpu.make_async_copy(grid.at[:, lons - HALO :], held.at[1], sems.at[1])
    west.start()
    east.start()
    west.wait()
    east.wait()

    def put(out, side):
        out[0] = near[side, :]
        for i in range(lats):
            out[i + 1] = held[0 if side.start == 0 else 1, i]
        out[lats + 1] = far[side, :]

    first, last = slice(0, HALO), slice(lons - HALO, lons)

    @pl.when(even)
    def _():
        put(near_out, last)
        put(far_out, first)

    @pl.when(jnp.logical_not(even))
    def _():
        put(near_out, first)
        put(far_out, last)


def places(source, lats, lons):
    band, sector = lax.axis_index("gx"), lax.axis_index("gy")
    lon_total = lons * lax.axis_size("gy")
    lat = (source >> log2(lon_total)) - band * lats + 1
    outer = (lat == 0) | (lat == lats + 1)
    lat = jnp.where(outer & (lax.rem(band, 2) == 0), lats + 1 - lat, lat)
    lon = ((source & (lon_total - 1)) - sector * lons + HALO) & (lon_total - 1)
    inner = (lon >= HALO) & (lon < HALO + lons)
    return lat, lon, inner


def gather_kernel(
    far, grid, near, mesh, w_message, w_update, w_next, source, target, next_source, next_target,
    partial, spread_out, mesh_out, w_out, sides_out, slots_out, order_out,
    held, indices, rows_held, table, sems,
):
    pairs = [(source, indices.at[0]), (target, indices.at[1])]
    pairs += [(grid, held), (w_message, w_out.at[0]), (mesh, mesh_out)]
    pairs += [(next_source, indices.at[2]), (next_target, indices.at[3])]
    pairs += [(w_update, w_out.at[1]), (w_next, w_out.at[2])]
    copies = [pltpu.make_async_copy(a, b, sems.at[i]) for i, (a, b) in enumerate(pairs)]
    for copy in copies:
        copy.start()
    lats, lons, width = grid.shape
    nodes = mesh.shape[0]
    copies[0].wait()
    copies[1].wait()
    lat, lon, inner = places(indices[0], lats, lons)
    src = jnp.where(inner, lat * lons + lon - HALO, -1)
    tgt = indices[1]
    edges = src.shape[0] * LANES
    spread_out[...] = spread(tgt, nodes)
    copies[2].wait()
    copies[3].wait()
    w = w_out[0]
    table[:lons, :] = dot(near[...], w).astype(jnp.bfloat16)
    inside = held[...].reshape(lats * lons, width)
    table[lons : (lats + 1) * lons, :] = dot(inside, w).astype(jnp.bfloat16)
    table[(lats + 1) * lons :, :] = dot(far[...], w).astype(jnp.bfloat16)
    copies[4].wait()
    depth = table.shape[0]
    side = (lats + 2) * HALO
    on_mate = (lon >= HALO) == (lax.rem(lax.axis_index("gy"), 2) == 0)
    edge = jnp.where(on_mate, 0, side) + lat * HALO + (lon & (HALO - 1))
    edge = jnp.where(inner, -1, edge)
    for c in range(0, edges, CHUNK):
        rows = slice(c, c + CHUNK)
        acc = dot(pick(column(src, rows), depth), table[...])
        partial[rows, :] = acc + dot(pick(column(tgt, rows), nodes), mesh_out[...])
        sides_out[rows, :] = pick(column(edge, rows), sides_out.shape[1])
    copies[5].wait()
    copies[6].wait()
    apart(indices.at[2], slots_out)
    apart(indices.at[3], rows_held)
    order_out[...] = together(rows_held)
    copies[7].wait()
    copies[8].wait()


def encode_kernel(
    partial, other, mate, spreading, mesh, weights, sides,
    first_out, next_out, table, messages,
):
    w = weights[0]
    tall, halo, width = mate.shape
    side = tall * halo
    table[:side, :] = dot(mate[...].reshape(side, width), w).astype(jnp.bfloat16)
    table[side : 2 * side, :] = dot(other[...].reshape(side, width), w).astype(jnp.bfloat16)
    table[2 * side :, :] = jnp.zeros((table.shape[0] - 2 * side, width), jnp.bfloat16)
    edges = partial.shape[0]
    for c in range(0, edges, CHUNK):
        rows = slice(c, c + CHUNK)
        messages[rows, :] = message(partial[rows, :] + dot(sides[rows, :], table[...]))
    summed = dot(spreading[...], messages[...])
    first = refresh(mesh[...], summed, weights[1])
    first_out[...] = first
    next_out[...] = dot(first, weights[2]).astype(jnp.bfloat16)


def request_kernel(table, mirror, slots, send_out):
    nodes = table.shape[0]
    asked = together(slots)
    lane = lax.broadcasted_iota(jnp.int32, asked.shape, 1)
    asked = asked + jnp.where((lane & (2 * CAP - 1)) >= CAP, nodes, 0)
    for c in range(0, send_out.shape[0], CHUNK):
        rows = slice(c, c + CHUNK)
        col = column(asked, rows)
        acc = dot(pick(col, nodes), table[...]) + dot(pick(col - nodes, nodes), mirror[...])
        send_out[rows, :] = acc.astype(jnp.bfloat16)


def target_kernel(first, target, w_update, w_next, partial, spread_out, w_out, sems):
    pairs = ((w_update, w_out.at[0]), (w_next, w_out.at[1]))
    copies = [pltpu.make_async_copy(a, b, sems.at[i]) for i, (a, b) in enumerate(pairs)]
    for copy in copies:
        copy.start()
    nodes = first.shape[0]
    tgt = target[...]
    for c in range(0, partial.shape[0], CHUNK):
        rows = slice(c, c + CHUNK)
        partial[rows, :] = dot(pick(column(tgt, rows), nodes), first[...])
    spread_out[...] = spread(tgt, nodes)
    for copy in copies:
        copy.wait()


def process_kernel(
    picked, partial, spreading, first, weights, second_out, table_out, messages
):
    for c in range(0, picked.shape[0], CHUNK):
        rows = slice(c, c + CHUNK)
        messages[rows, :] = message(partial[rows, :] + picked[rows, :].astype(jnp.float32))
    second = refresh(first[...], dot(spreading[...], messages[...]), weights[0])
    second_out[...] = second
    table_out[...] = dot(second, weights[1]).astype(jnp.bfloat16)


def reach_kernel(
    own, grid, source, target, w_update, partial, picks_out, spread_out, w_out, sem
):
    copy = pltpu.make_async_copy(w_update, w_out, sem)
    copy.start()
    latent = grid[...]
    cells = latent.shape[0]
    nodes = own.shape[0]
    src, tgt = source[...], target[...]
    for c in range(0, partial.shape[0], CHUNK):
        rows = slice(c, c + CHUNK)
        col = column(src, rows)
        acc = dot(pick(column(tgt, rows), cells), latent)
        partial[rows, :] = acc + dot(pick(col, nodes), own[...])
        picks_out[rows, :] = pick(col - nodes, 2 * nodes)
    spread_out[...] = spread(tgt, cells)
    copy.wait()


def decode_kernel(
    partial, other, mate, picks, spreading, grid, w_update, grid_out, messages
):
    nodes = mate.shape[0]
    for c in range(0, partial.shape[0], CHUNK):
        rows = slice(c, c + CHUNK)
        acc = partial[rows, :] + dot(picks[rows, :nodes], mate[...])
        messages[rows, :] = message(acc + dot(picks[rows, nodes:], other[...]))
    summed = dot(spreading[...], messages[...])
    grid_out[...] = refresh(grid[...], summed, w_update[...])


def on_device(
    grid_latent,
    mesh_latent,
    encode_message,
    encode_update,
    process_message,
    process_update,
    decode_message,
    decode_update,
    encode_source,
    encode_target,
    process_source,
    process_target,
    decode_source,
    decode_target,
):
    lat_rows, lon_cols, width = grid_latent.shape
    bands = lax.axis_size("gx")
    sectors = lax.axis_size("gy")
    sector = lax.axis_index("gy")
    mesh_rows = mesh_latent.reshape(-1, width)
    nodes = mesh_rows.shape[0]
    grid_rows = grid_latent.reshape(-1, width)
    cells = grid_rows.shape[0]
    edges = encode_source.size
    bf16 = jnp.bfloat16
    params = pltpu.CompilerParams(vmem_limit_bytes=40 * 1024 * 1024)
    hbm = pl.BlockSpec(memory_space=pltpu.HBM)
    vmem = pl.BlockSpec(memory_space=pltpu.VMEM)
    assert lon_cols == LON_DEV

    def pinned(array):
        return pltpu.with_memory_space_constraint(array, pltpu.HBM)

    partner = [i + 1 if i % 2 else i - 1 for i in range(max(bands, sectors))]
    far_bands = [(i, partner[i]) for i in range(1, bands - 1)]
    near_bands = [(i, i ^ 1) for i in range(bands)]
    far_sectors = [(i, partner[i] % sectors) for i in range(sectors)]
    near_sectors = [(i, i ^ 1) for i in range(sectors)]

    group = [[i for i in range(sectors) if i // HALF % 2 == h] for h in range(2)]

    def exchange(array):
        return lax.all_to_all(array, "gy", 0, 0, axis_index_groups=group, tiled=True)

    band_edge = jax.ShapeDtypeStruct((lon_cols, width), bf16)
    far, near = pl.pallas_call(
        edges_kernel,
        in_specs=[hbm],
        out_specs=(vmem,) * 2,
        out_shape=(band_edge,) * 2,
        scratch_shapes=[pltpu.SemaphoreType.DMA((2,))],
        compiler_params=params,
    )(pinned(grid_latent))
    far = lax.ppermute(far, "gx", far_bands)
    near = lax.ppermute(near, "gx", near_bands)
    sector_edge = jax.ShapeDtypeStruct((lat_rows + 2, HALO, width), bf16)
    other, mate = pl.pallas_call(
        sides_kernel,
        in_specs=[vmem, hbm, vmem],
        out_specs=(vmem,) * 2,
        out_shape=(sector_edge,) * 2,
        scratch_shapes=[
            pltpu.VMEM((2, lat_rows, HALO, width), bf16),
            pltpu.SemaphoreType.DMA((2,)),
        ],
        compiler_params=params,
    )(far, pinned(grid_latent), near)
    other = lax.ppermute(other, "gy", far_sectors)
    mate = lax.ppermute(mate, "gy", near_sectors)

    tall_cells = (lat_rows + 2) * lon_cols
    depth = -(-2 * (lat_rows + 2) * HALO // LANES) * LANES
    index = jax.ShapeDtypeStruct((edges // LANES, LANES), jnp.int32)
    table_shape = jax.ShapeDtypeStruct((nodes, width), bf16)
    partial_shape = jax.ShapeDtypeStruct((edges, width), jnp.float32)
    spread_shape = jax.ShapeDtypeStruct((nodes, edges), bf16)
    slots_shape = jax.ShapeDtypeStruct((sectors // 2, LANES), jnp.int32)
    partial, spreading, mesh_held, weights, sides, slots, order = pl.pallas_call(
        gather_kernel,
        in_specs=[vmem, hbm, vmem] + [hbm] * 8,
        out_specs=(vmem,) * 7,
        out_shape=(
            partial_shape,
            spread_shape,
            table_shape,
            jax.ShapeDtypeStruct((3, width, width), bf16),
            jax.ShapeDtypeStruct((edges, depth), bf16),
            slots_shape,
            index,
        ),
        scratch_shapes=[
            pltpu.VMEM((lat_rows, lon_cols, width), bf16),
            pltpu.VMEM((4, edges // LANES, LANES), jnp.int32),
            pltpu.VMEM(slots_shape.shape, jnp.int32),
            pltpu.VMEM((tall_cells, width), bf16),
            pltpu.SemaphoreType.DMA((9,)),
        ],
        compiler_params=params,
    )(
        far, pinned(grid_latent), near, pinned(mesh_rows), pinned(encode_message),
        pinned(encode_update), pinned(process_message),
        *(
            pinned(array.reshape(-1, LANES))
            for array in (encode_source, encode_target, process_source, process_target)
        ),
    )
    messages = pltpu.VMEM((edges, width), bf16)
    first, following = pl.pallas_call(
        encode_kernel,
        out_shape=(table_shape, table_shape),
        scratch_shapes=[pltpu.VMEM((depth, width), bf16), messages],
        compiler_params=params,
    )(partial, other, mate, spreading, mesh_held, weights, sides)

    following, slots = lax.optimization_barrier((following, slots))
    mirror = lax.ppermute(following, "gy", [(i, i ^ HALF) for i in range(sectors)])
    slots = exchange(slots)
    partial, spreading, weights = pl.pallas_call(
        target_kernel,
        in_specs=[vmem] * 2 + [hbm] * 2,
        out_specs=(vmem,) * 3,
        out_shape=(
            partial_shape, spread_shape, jax.ShapeDtypeStruct((2, width, width), bf16)
        ),
        scratch_shapes=[pltpu.SemaphoreType.DMA((2,))],
        compiler_params=params,
    )(first, order, pinned(process_update), pinned(decode_message))
    send = pl.pallas_call(
        request_kernel,
        out_shape=jax.ShapeDtypeStruct((edges, width), bf16),
        compiler_params=params,
    )(following, mirror, slots)
    picked = exchange(send.reshape(sectors // 2, -1, width)).reshape(edges, width)
    second, table = pl.pallas_call(
        process_kernel,
        out_shape=(table_shape, table_shape),
        scratch_shapes=[messages],
        compiler_params=params,
    )(picked, partial, spreading, first, weights)

    other = lax.ppermute(table, "gy", far_sectors)
    mate = lax.ppermute(table, "gy", near_sectors)
    source = decode_source.reshape(-1, LANES)
    owner = source // nodes % sectors
    piece = jnp.where(owner == sector, 0, jnp.where(owner == sector ^ 1, 1, 2))
    row = piece * nodes + source % nodes
    target = decode_target.reshape(-1, LANES)
    partial, picks, spreading, update = pl.pallas_call(
        reach_kernel,
        in_specs=[vmem] * 4 + [hbm],
        out_specs=(vmem,) * 4,
        out_shape=(
            partial_shape,
            jax.ShapeDtypeStruct((edges, 2 * nodes), bf16),
            jax.ShapeDtypeStruct((cells, edges), bf16),
            jax.ShapeDtypeStruct((width, width), bf16),
        ),
        scratch_shapes=[pltpu.SemaphoreType.DMA(())],
        compiler_params=params,
    )(table, grid_rows, row, target, pinned(decode_update))
    grid_output = pl.pallas_call(
        decode_kernel,
        out_shape=jax.ShapeDtypeStruct((cells, width), bf16),
        scratch_shapes=[messages],
        compiler_params=params,
    )(partial, other, mate, picks, spreading, grid_rows, update)
    return (
        grid_output.reshape(lat_rows, lon_cols, width),
        second.reshape(1, 1, nodes, width),
    )


def solution(mesh):
    edge = P("gx", "gy", None)
    return jax.shard_map(
        on_device,
        mesh=mesh,
        in_specs=(
            P("gx", "gy", None),
            P("gx", "gy", None, None),
            *([P()] * 6),
            *([edge] * 6),
        ),
        out_specs=(P("gx", "gy", None), P("gx", "gy", None, None)),
        check_vma=False,
    )
```

```python
import jax
import jax.numpy as jnp
from jax import lax
from jax.experimental import pallas as pl
from jax.experimental.pallas import tpu as pltpu
from jax.sharding import PartitionSpec as P

HALO = 8
LON_DEV = 64
EPSILON = 1e-05
LANES = 128
CHUNK = 256
CAP = 16
GROUPS = LANES // CAP
HALF = 8


def column(index, rows):
    parts = []
    for i in range(rows.start // LANES, rows.stop // LANES):
        row = jnp.broadcast_to(index[i : i + 1, :], (LANES, LANES))
        parts.append(row.T)
    return jnp.concatenate(parts, axis=0)


def pick(col, count):
    lane = lax.broadcasted_iota(jnp.int32, col.shape, 1)
    parts = [
        jnp.where(col == lane + k, 1.0, 0.0).astype(jnp.bfloat16)
        for k in range(0, count, LANES)
    ]
    return jnp.concatenate(parts, axis=1)


def spread(index, count):
    sub = lax.broadcasted_iota(jnp.int32, (count, LANES), 0)
    parts = [
        jnp.where(index[i : i + 1, :] == sub, 1.0, 0.0).astype(jnp.bfloat16)
        for i in range(index.shape[0])
    ]
    return jnp.concatenate(parts, axis=1)


def dot(a, b):
    return jnp.dot(a, b, preferred_element_type=jnp.float32)


def message(summed):
    half = 0.5 * summed
    return (half * jnp.tanh(half) + half).astype(jnp.bfloat16)


def refresh(latent, summed, weight):
    scaled = summed * lax.rsqrt(jnp.mean(summed * summed, axis=-1, keepdims=True) + EPSILON)
    return (latent.astype(jnp.float32) + dot(scaled.astype(jnp.bfloat16), weight)).astype(
        jnp.bfloat16
    )


def log2(value):
    assert value & (value - 1) == 0
    return value.bit_length() - 1


def roll(value, shift):
    return pltpu.roll(value, shift % LANES, 1) if shift % LANES else value


def halves(index):
    upper = lax.rem(lax.axis_index("gy") // HALF, 2) == 1
    count = index.shape[0] // 2
    low = index[pl.ds(0, count, stride=2), :]
    high = index[pl.ds(1, count, stride=2), :]
    return jnp.where(upper, high, low), jnp.where(upper, low, high)


def apart(slots, out):
    own, mirror = halves(slots)
    lane = lax.broadcasted_iota(jnp.int32, own.shape, 1)
    for g in range(GROUPS):
        first = roll(own, -g * CAP)
        second = roll(mirror, CAP - g * CAP)
        out[pl.ds(g, own.shape[0], stride=GROUPS), :] = jnp.where(lane < CAP, first, second)


def together(rows):
    each = 2 * CAP
    fold = LANES // each
    count = rows.shape[0] // fold
    lane = lax.broadcasted_iota(jnp.int32, (count, LANES), 1)
    kept = jnp.zeros_like(lane)
    for g in range(fold):
        moved = roll(rows[pl.ds(g, count, stride=fold), :], g * each)
        kept = jnp.where((lane >= g * each) & (lane < (g + 1) * each), moved, kept)
    return kept


def edges_kernel(grid, far_out, near_out, sems):
    even = lax.rem(lax.axis_index("gx"), 2) == 0
    last = grid.shape[0] - 1
    near = pltpu.make_async_copy(grid.at[jnp.where(even, last, 0)], near_out, sems.at[0])
    far = pltpu.make_async_copy(grid.at[jnp.where(even, 0, last)], far_out, sems.at[1])
    near.start()
    far.start()
    near.wait()
    far.wait()


def sides_kernel(far, grid, near, far_out, near_out, held, sems):
    even = lax.rem(lax.axis_index("gy"), 2) == 0
    lats, lons, _ = grid.shape
    west = pltpu.make_async_copy(grid.at[:, :HALO], held.at[0], sems.at[0])
    east = pltpu.make_async_copy(grid.at[:, lons - HALO :], held.at[1], sems.at[1])
    west.start()
    east.start()
    west.wait()
    east.wait()

    def put(out, side):
        out[0] = near[side, :]
        for i in range(lats):
            out[i + 1] = held[0 if side.start == 0 else 1, i]
        out[lats + 1] = far[side, :]

    first, last = slice(0, HALO), slice(lons - HALO, lons)

    @pl.when(even)
    def _():
        put(near_out, last)
        put(far_out, first)

    @pl.when(jnp.logical_not(even))
    def _():
        put(near_out, first)
        put(far_out, last)


def places(source, lats, lons):
    band, sector = lax.axis_index("gx"), lax.axis_index("gy")
    lon_total = lons * lax.axis_size("gy")
    lat = (source >> log2(lon_total)) - band * lats + 1
    outer = (lat == 0) | (lat == lats + 1)
    lat = jnp.where(outer & (lax.rem(band, 2) == 0), lats + 1 - lat, lat)
    lon = ((source & (lon_total - 1)) - sector * lons + HALO) & (lon_total - 1)
    inner = (lon >= HALO) & (lon < HALO + lons)
    return lat, lon, inner


def gather_kernel(
    far, grid, near, mesh, w_message, w_update, w_next, source, target, next_source, next_target,
    partial, spread_out, mesh_out, w_out, sides_out, slots_out, order_out,
    held, indices, rows_held, table, sems,
):
    pairs = [(source, indices.at[0]), (target, indices.at[1])]
    pairs += [(grid, held), (w_message, w_out.at[0]), (mesh, mesh_out)]
    pairs += [(next_source, indices.at[2]), (next_target, indices.at[3])]
    pairs += [(w_update, w_out.at[1]), (w_next, w_out.at[2])]
    copies = [pltpu.make_async_copy(a, b, sems.at[i]) for i, (a, b) in enumerate(pairs)]
    for copy in copies:
        copy.start()
    lats, lons, width = grid.shape
    nodes = mesh.shape[0]
    copies[0].wait()
    copies[1].wait()
    lat, lon, inner = places(indices[0], lats, lons)
    src = jnp.where(inner, lat * lons + lon - HALO, -1)
    tgt = indices[1]
    edges = src.shape[0] * LANES
    spread_out[...] = spread(tgt, nodes)
    copies[2].wait()
    copies[3].wait()
    w = w_out[0]
    table[:lons, :] = dot(near[...], w).astype(jnp.bfloat16)
    inside = held[...].reshape(lats * lons, width)
    table[lons : (lats + 1) * lons, :] = dot(inside, w).astype(jnp.bfloat16)
    table[(lats + 1) * lons :, :] = dot(far[...], w).astype(jnp.bfloat16)
    copies[4].wait()
    depth = table.shape[0]
    side = (lats + 2) * HALO
    on_mate = (lon >= HALO) == (lax.rem(lax.axis_index("gy"), 2) == 0)
    edge = jnp.where(on_mate, 0, side) + lat * HALO + (lon & (HALO - 1))
    edge = jnp.where(inner, -1, edge)
    for c in range(0, edges, CHUNK):
        rows = slice(c, c + CHUNK)
        acc = dot(pick(column(src, rows), depth), table[...])
        partial[rows, :] = acc + dot(pick(column(tgt, rows), nodes), mesh_out[...])
        sides_out[rows, :] = pick(column(edge, rows), sides_out.shape[1])
    copies[5].wait()
    copies[6].wait()
    apart(indices.at[2], slots_out)
    apart(indices.at[3], rows_held)
    order_out[...] = together(rows_held)
    copies[7].wait()
    copies[8].wait()


def encode_kernel(
    partial, other, mate, spreading, mesh, weights, sides,
    first_out, next_out, table, messages,
):
    w = weights[0]
    tall, halo, width = mate.shape
    side = tall * halo
    table[:side, :] = dot(mate[...].reshape(side, width), w).astype(jnp.bfloat16)
    table[side : 2 * side, :] = dot(other[...].reshape(side, width), w).astype(jnp.bfloat16)
    table[2 * side :, :] = jnp.zeros((table.shape[0] - 2 * side, width), jnp.bfloat16)
    edges = partial.shape[0]
    for c in range(0, edges, CHUNK):
        rows = slice(c, c + CHUNK)
        messages[rows, :] = message(partial[rows, :] + dot(sides[rows, :], table[...]))
    summed = dot(spreading[...], messages[...])
    first = refresh(mesh[...], summed, weights[1])
    first_out[...] = first
    next_out[...] = dot(first, weights[2]).astype(jnp.bfloat16)


def request_kernel(table, mirror, slots, send_out):
    nodes = table.shape[0]
    asked = together(slots)
    lane = lax.broadcasted_iota(jnp.int32, asked.shape, 1)
    asked = asked + jnp.where((lane & (2 * CAP - 1)) >= CAP, nodes, 0)
    for c in range(0, send_out.shape[0], CHUNK):
        rows = slice(c, c + CHUNK)
        col = column(asked, rows)
        acc = dot(pick(col, nodes), table[...]) + dot(pick(col - nodes, nodes), mirror[...])
        send_out[rows, :] = acc.astype(jnp.bfloat16)


def process_kernel(
    picked, target, first, w_update, w_next, second_out, table_out, messages
):
    nodes = first.shape[0]
    tgt = target[...]
    for c in range(0, picked.shape[0], CHUNK):
        rows = slice(c, c + CHUNK)
        acc = dot(pick(column(tgt, rows), nodes), first[...])
        messages[rows, :] = message(acc + picked[rows, :].astype(jnp.float32))
    second = refresh(first[...], dot(spread(tgt, nodes), messages[...]), w_update[...])
    second_out[...] = second
    table_out[...] = dot(second, w_next[...]).astype(jnp.bfloat16)


def reach_kernel(
    own, grid, source, target, w_update, partial, picks_out, spread_out, w_out, sem
):
    copy = pltpu.make_async_copy(w_update, w_out, sem)
    copy.start()
    latent = grid[...]
    cells = latent.shape[0]
    nodes = own.shape[0]
    src, tgt = source[...], target[...]
    for c in range(0, partial.shape[0], CHUNK):
        rows = slice(c, c + CHUNK)
        col = column(src, rows)
        acc = dot(pick(column(tgt, rows), cells), latent)
        partial[rows, :] = acc + dot(pick(col, nodes), own[...])
        picks_out[rows, :] = pick(col - nodes, 2 * nodes)
    spread_out[...] = spread(tgt, cells)
    copy.wait()


def decode_kernel(
    partial, other, mate, picks, spreading, grid, w_update, grid_out, messages
):
    nodes = mate.shape[0]
    for c in range(0, partial.shape[0], CHUNK):
        rows = slice(c, c + CHUNK)
        acc = partial[rows, :] + dot(picks[rows, :nodes], mate[...])
        messages[rows, :] = message(acc + dot(picks[rows, nodes:], other[...]))
    summed = dot(spreading[...], messages[...])
    grid_out[...] = refresh(grid[...], summed, w_update[...])


def on_device(
    grid_latent,
    mesh_latent,
    encode_message,
    encode_update,
    process_message,
    process_update,
    decode_message,
    decode_update,
    encode_source,
    encode_target,
    process_source,
    process_target,
    decode_source,
    decode_target,
):
    lat_rows, lon_cols, width = grid_latent.shape
    bands = lax.axis_size("gx")
    sectors = lax.axis_size("gy")
    sector = lax.axis_index("gy")
    mesh_rows = mesh_latent.reshape(-1, width)
    nodes = mesh_rows.shape[0]
    grid_rows = grid_latent.reshape(-1, width)
    cells = grid_rows.shape[0]
    edges = encode_source.size
    bf16 = jnp.bfloat16
    params = pltpu.CompilerParams(vmem_limit_bytes=40 * 1024 * 1024)
    hbm = pl.BlockSpec(memory_space=pltpu.HBM)
    vmem = pl.BlockSpec(memory_space=pltpu.VMEM)
    assert lon_cols == LON_DEV

    def pinned(array):
        return pltpu.with_memory_space_constraint(array, pltpu.HBM)

    partner = [i + 1 if i % 2 else i - 1 for i in range(max(bands, sectors))]
    far_bands = [(i, partner[i]) for i in range(1, bands - 1)]
    near_bands = [(i, i ^ 1) for i in range(bands)]
    far_sectors = [(i, partner[i] % sectors) for i in range(sectors)]
    near_sectors = [(i, i ^ 1) for i in range(sectors)]

    group = [[i for i in range(sectors) if i // HALF % 2 == h] for h in range(2)]

    def exchange(array):
        return lax.all_to_all(array, "gy", 0, 0, axis_index_groups=group, tiled=True)

    band_edge = jax.ShapeDtypeStruct((lon_cols, width), bf16)
    far, near = pl.pallas_call(
        edges_kernel,
        in_specs=[hbm],
        out_specs=(vmem,) * 2,
        out_shape=(band_edge,) * 2,
        scratch_shapes=[pltpu.SemaphoreType.DMA((2,))],
        compiler_params=params,
    )(pinned(grid_latent))
    far = lax.ppermute(far, "gx", far_bands)
    near = lax.ppermute(near, "gx", near_bands)
    sector_edge = jax.ShapeDtypeStruct((lat_rows + 2, HALO, width), bf16)
    other, mate = pl.pallas_call(
        sides_kernel,
        in_specs=[vmem, hbm, vmem],
        out_specs=(vmem,) * 2,
        out_shape=(sector_edge,) * 2,
        scratch_shapes=[
            pltpu.VMEM((2, lat_rows, HALO, width), bf16),
            pltpu.SemaphoreType.DMA((2,)),
        ],
        compiler_params=params,
    )(far, pinned(grid_latent), near)
    other = lax.ppermute(other, "gy", far_sectors)
    mate = lax.ppermute(mate, "gy", near_sectors)

    tall_cells = (lat_rows + 2) * lon_cols
    depth = -(-2 * (lat_rows + 2) * HALO // LANES) * LANES
    index = jax.ShapeDtypeStruct((edges // LANES, LANES), jnp.int32)
    table_shape = jax.ShapeDtypeStruct((nodes, width), bf16)
    partial_shape = jax.ShapeDtypeStruct((edges, width), jnp.float32)
    spread_shape = jax.ShapeDtypeStruct((nodes, edges), bf16)
    slots_shape = jax.ShapeDtypeStruct((sectors // 2, LANES), jnp.int32)
    partial, spreading, mesh_held, weights, sides, slots, order = pl.pallas_call(
        gather_kernel,
        in_specs=[vmem, hbm, vmem] + [hbm] * 8,
        out_specs=(vmem,) * 7,
        out_shape=(
            partial_shape,
            spread_shape,
            table_shape,
            jax.ShapeDtypeStruct((3, width, width), bf16),
            jax.ShapeDtypeStruct((edges, depth), bf16),
            slots_shape,
            index,
        ),
        scratch_shapes=[
            pltpu.VMEM((lat_rows, lon_cols, width), bf16),
            pltpu.VMEM((4, edges // LANES, LANES), jnp.int32),
            pltpu.VMEM(slots_shape.shape, jnp.int32),
            pltpu.VMEM((tall_cells, width), bf16),
            pltpu.SemaphoreType.DMA((9,)),
        ],
        compiler_params=params,
    )(
        far, pinned(grid_latent), near, pinned(mesh_rows), pinned(encode_message),
        pinned(encode_update), pinned(process_message),
        *(
            pinned(array.reshape(-1, LANES))
            for array in (encode_source, encode_target, process_source, process_target)
        ),
    )
    messages = pltpu.VMEM((edges, width), bf16)
    first, following = pl.pallas_call(
        encode_kernel,
        out_shape=(table_shape, table_shape),
        scratch_shapes=[pltpu.VMEM((depth, width), bf16), messages],
        compiler_params=params,
    )(partial, other, mate, spreading, mesh_held, weights, sides)

    following, slots = lax.optimization_barrier((following, slots))
    mirror = lax.ppermute(following, "gy", [(i, i ^ HALF) for i in range(sectors)])
    slots = exchange(slots)
    send = pl.pallas_call(
        request_kernel,
        out_shape=jax.ShapeDtypeStruct((edges, width), bf16),
        compiler_params=params,
    )(following, mirror, slots)
    picked = exchange(send.reshape(sectors // 2, -1, width)).reshape(edges, width)
    second, table = pl.pallas_call(
        process_kernel,
        out_shape=(table_shape, table_shape),
        scratch_shapes=[messages],
        compiler_params=params,
    )(picked, order, first, process_update, decode_message)

    other = lax.ppermute(table, "gy", far_sectors)
    mate = lax.ppermute(table, "gy", near_sectors)
    source = decode_source.reshape(-1, LANES)
    owner = source // nodes % sectors
    piece = jnp.where(owner == sector, 0, jnp.where(owner == sector ^ 1, 1, 2))
    row = piece * nodes + source % nodes
    target = decode_target.reshape(-1, LANES)
    partial, picks, spreading, update = pl.pallas_call(
        reach_kernel,
        in_specs=[vmem] * 4 + [hbm],
        out_specs=(vmem,) * 4,
        out_shape=(
            partial_shape,
            jax.ShapeDtypeStruct((edges, 2 * nodes), bf16),
            jax.ShapeDtypeStruct((cells, edges), bf16),
            jax.ShapeDtypeStruct((width, width), bf16),
        ),
        scratch_shapes=[pltpu.SemaphoreType.DMA(())],
        compiler_params=params,
    )(table, grid_rows, row, target, pinned(decode_update))
    grid_output = pl.pallas_call(
        decode_kernel,
        out_shape=jax.ShapeDtypeStruct((cells, width), bf16),
        scratch_shapes=[messages],
        compiler_params=params,
    )(partial, other, mate, picks, spreading, grid_rows, update)
    return (
        grid_output.reshape(lat_rows, lon_cols, width),
        second.reshape(1, 1, nodes, width),
    )


def solution(mesh):
    edge = P("gx", "gy", None)
    return jax.shard_map(
        on_device,
        mesh=mesh,
        in_specs=(
            P("gx", "gy", None),
            P("gx", "gy", None, None),
            *([P()] * 6),
            *([edge] * 6),
        ),
        out_specs=(P("gx", "gy", None), P("gx", "gy", None, None)),
        check_vma=False,
    )
```

```python
import jax
import jax.numpy as jnp
from jax import lax
from jax.experimental import pallas as pl
from jax.experimental.pallas import tpu as pltpu
from jax.sharding import PartitionSpec as P

HALO = 8
LON_DEV = 64
EPSILON = 1e-05
LANES = 128
CHUNK = 256
CAP = 16
GROUPS = LANES // CAP
HALF = 8
CORES = 2
PLANES = HALF // CORES


def column(index, rows):
    parts = []
    for i in range(rows.start // LANES, rows.stop // LANES):
        row = jnp.broadcast_to(index[i : i + 1, :], (LANES, LANES))
        parts.append(row.T)
    return jnp.concatenate(parts, axis=0)


def pick(col, count):
    lane = lax.broadcasted_iota(jnp.int32, col.shape, 1)
    parts = [
        jnp.where(col == lane + k, 1.0, 0.0).astype(jnp.bfloat16)
        for k in range(0, count, LANES)
    ]
    return jnp.concatenate(parts, axis=1)


def spread(index, count):
    sub = lax.broadcasted_iota(jnp.int32, (count, LANES), 0)
    parts = [
        jnp.where(index[i : i + 1, :] == sub, 1.0, 0.0).astype(jnp.bfloat16)
        for i in range(index.shape[0])
    ]
    return jnp.concatenate(parts, axis=1)


def dot(a, b):
    return jnp.dot(a, b, preferred_element_type=jnp.float32)


def message(summed):
    half = 0.5 * summed
    return (half * jnp.tanh(half) + half).astype(jnp.bfloat16)


def refresh(latent, summed, weight):
    scaled = summed * lax.rsqrt(jnp.mean(summed * summed, axis=-1, keepdims=True) + EPSILON)
    return (latent.astype(jnp.float32) + dot(scaled.astype(jnp.bfloat16), weight)).astype(
        jnp.bfloat16
    )


def log2(value):
    assert value & (value - 1) == 0
    return value.bit_length() - 1


def roll(value, shift):
    return pltpu.roll(value, shift % LANES, 1) if shift % LANES else value


def halves(index):
    upper = lax.rem(lax.axis_index("gy") // HALF, 2) == 1
    count = index.shape[0] // 2
    low = index[pl.ds(0, count, stride=2), :]
    high = index[pl.ds(1, count, stride=2), :]
    return jnp.where(upper, high, low), jnp.where(upper, low, high)


def apart(slots, out):
    own, mirror = halves(slots)
    lane = lax.broadcasted_iota(jnp.int32, own.shape, 1)
    for g in range(GROUPS):
        first = roll(own, -g * CAP)
        second = roll(mirror, CAP - g * CAP)
        out[pl.ds(g, own.shape[0], stride=GROUPS), :] = jnp.where(lane < CAP, first, second)


def together(rows):
    each = 2 * CAP
    fold = LANES // each
    count = rows.shape[0] // fold
    lane = lax.broadcasted_iota(jnp.int32, (count, LANES), 1)
    kept = jnp.zeros_like(lane)
    for g in range(fold):
        moved = roll(rows[pl.ds(g, count, stride=fold), :], g * each)
        kept = jnp.where((lane >= g * each) & (lane < (g + 1) * each), moved, kept)
    return kept


def by_plane(rows, out):
    count = rows.shape[0] // HALF
    each = 2 * CAP
    lane = lax.broadcasted_iota(jnp.int32, (count, LANES), 1)
    for core in range(CORES):
        kept = jnp.zeros_like(lane)
        for p in range(PLANES):
            moved = roll(rows[pl.ds(p * CORES + core, count, stride=HALF), :], p * each)
            kept = jnp.where((lane >= p * each) & (lane < (p + 1) * each), moved, kept)
        out[pl.ds(core, count, stride=CORES), :] = kept


def planes_kernel(slots, slots_out):
    count = slots.shape[0]
    for p in range(PLANES):
        slots_out[p * count : (p + 1) * count, :] = roll(slots[...], -p * 2 * CAP)


def edges_kernel(grid, far_out, near_out, sems):
    even = lax.rem(lax.axis_index("gx"), 2) == 0
    last = grid.shape[0] - 1
    near = pltpu.make_async_copy(grid.at[jnp.where(even, last, 0)], near_out, sems.at[0])
    far = pltpu.make_async_copy(grid.at[jnp.where(even, 0, last)], far_out, sems.at[1])
    near.start()
    far.start()
    near.wait()
    far.wait()


def sides_kernel(far, grid, near, far_out, near_out, held, sems):
    even = lax.rem(lax.axis_index("gy"), 2) == 0
    lats, lons, _ = grid.shape
    west = pltpu.make_async_copy(grid.at[:, :HALO], held.at[0], sems.at[0])
    east = pltpu.make_async_copy(grid.at[:, lons - HALO :], held.at[1], sems.at[1])
    west.start()
    east.start()
    west.wait()
    east.wait()

    def put(out, side):
        out[0] = near[side, :]
        for i in range(lats):
            out[i + 1] = held[0 if side.start == 0 else 1, i]
        out[lats + 1] = far[side, :]

    first, last = slice(0, HALO), slice(lons - HALO, lons)

    @pl.when(even)
    def _():
        put(near_out, last)
        put(far_out, first)

    @pl.when(jnp.logical_not(even))
    def _():
        put(near_out, first)
        put(far_out, last)


def places(source, lats, lons):
    band, sector = lax.axis_index("gx"), lax.axis_index("gy")
    lon_total = lons * lax.axis_size("gy")
    lat = (source >> log2(lon_total)) - band * lats + 1
    outer = (lat == 0) | (lat == lats + 1)
    lat = jnp.where(outer & (lax.rem(band, 2) == 0), lats + 1 - lat, lat)
    lon = ((source & (lon_total - 1)) - sector * lons + HALO) & (lon_total - 1)
    inner = (lon >= HALO) & (lon < HALO + lons)
    return lat, lon, inner


def gather_kernel(
    far, grid, near, mesh, w_message, w_update, w_next, source, target, next_source, next_target,
    partial, spread_out, mesh_out, w_out, sides_out, slots_out, order_out,
    held, indices, rows_held, table, sems,
):
    pairs = [(source, indices.at[0]), (target, indices.at[1])]
    pairs += [(grid, held), (w_message, w_out.at[0]), (mesh, mesh_out)]
    pairs += [(next_source, indices.at[2]), (next_target, indices.at[3])]
    pairs += [(w_update, w_out.at[1]), (w_next, w_out.at[2])]
    copies = [pltpu.make_async_copy(a, b, sems.at[i]) for i, (a, b) in enumerate(pairs)]
    for copy in copies:
        copy.start()
    lats, lons, width = grid.shape
    nodes = mesh.shape[0]
    copies[0].wait()
    copies[1].wait()
    lat, lon, inner = places(indices[0], lats, lons)
    src = jnp.where(inner, lat * lons + lon - HALO, -1)
    tgt = indices[1]
    edges = src.shape[0] * LANES
    spread_out[...] = spread(tgt, nodes)
    copies[2].wait()
    copies[3].wait()
    w = w_out[0]
    table[:lons, :] = dot(near[...], w).astype(jnp.bfloat16)
    inside = held[...].reshape(lats * lons, width)
    table[lons : (lats + 1) * lons, :] = dot(inside, w).astype(jnp.bfloat16)
    table[(lats + 1) * lons :, :] = dot(far[...], w).astype(jnp.bfloat16)
    copies[4].wait()
    depth = table.shape[0]
    side = (lats + 2) * HALO
    on_mate = (lon >= HALO) == (lax.rem(lax.axis_index("gy"), 2) == 0)
    edge = jnp.where(on_mate, 0, side) + lat * HALO + (lon & (HALO - 1))
    edge = jnp.where(inner, -1, edge)
    for c in range(0, edges, CHUNK):
        rows = slice(c, c + CHUNK)
        acc = dot(pick(column(src, rows), depth), table[...])
        partial[rows, :] = acc + dot(pick(column(tgt, rows), nodes), mesh_out[...])
        sides_out[rows, :] = pick(column(edge, rows), sides_out.shape[1])
    copies[5].wait()
    copies[6].wait()
    apart(indices.at[2], rows_held)
    by_plane(rows_held, slots_out)
    apart(indices.at[3], rows_held)
    order_out[...] = together(rows_held)
    copies[7].wait()
    copies[8].wait()


def encode_kernel(
    partial, other, mate, spreading, mesh, weights, sides,
    first_out, next_out, table, messages,
):
    w = weights[0]
    tall, halo, width = mate.shape
    side = tall * halo
    table[:side, :] = dot(mate[...].reshape(side, width), w).astype(jnp.bfloat16)
    table[side : 2 * side, :] = dot(other[...].reshape(side, width), w).astype(jnp.bfloat16)
    table[2 * side :, :] = jnp.zeros((table.shape[0] - 2 * side, width), jnp.bfloat16)
    edges = partial.shape[0]
    for c in range(0, edges, CHUNK):
        rows = slice(c, c + CHUNK)
        messages[rows, :] = message(partial[rows, :] + dot(sides[rows, :], table[...]))
    summed = dot(spreading[...], messages[...])
    first = refresh(mesh[...], summed, weights[1])
    first_out[...] = first
    next_out[...] = dot(first, weights[2]).astype(jnp.bfloat16)


def request_kernel(table, mirror, slots, send_out, held):
    nodes = table.shape[0]
    plane = slots.shape[0] // PLANES
    count = plane // CORES
    for p in range(PLANES):
        for core in range(CORES):
            part = slots[pl.ds(p * plane + core, count, stride=CORES), :]
            held[pl.ds(p * CORES + core, count, stride=HALF), :] = part
    asked = together(held)
    lane = lax.broadcasted_iota(jnp.int32, asked.shape, 1)
    asked = asked + jnp.where((lane & (2 * CAP - 1)) >= CAP, nodes, 0)
    for c in range(0, send_out.shape[0], CHUNK):
        rows = slice(c, c + CHUNK)
        col = column(asked, rows)
        acc = dot(pick(col, nodes), table[...]) + dot(pick(col - nodes, nodes), mirror[...])
        send_out[rows, :] = acc.astype(jnp.bfloat16)


def process_kernel(
    picked, target, first, w_update, w_next, second_out, table_out, messages, held, sem
):
    nodes = first.shape[0]
    tgt = target[...]
    for c in range(0, picked.shape[0], CHUNK):
        rows = slice(c, c + CHUNK)
        acc = dot(pick(column(tgt, rows), nodes), first[...])
        messages[rows, :] = message(acc + picked[rows, :].astype(jnp.float32))
    second = refresh(first[...], dot(spread(tgt, nodes), messages[...]), w_update[...])
    held[...] = second
    copy = pltpu.make_async_copy(held, second_out, sem)
    copy.start()
    table_out[...] = dot(second, w_next[...]).astype(jnp.bfloat16)
    copy.wait()


def reach_kernel(
    own, grid, source, target, w_update, partial, picks_out, spread_out, w_out, sem
):
    copy = pltpu.make_async_copy(w_update, w_out, sem)
    copy.start()
    latent = grid[...]
    cells = latent.shape[0]
    nodes = own.shape[0]
    src, tgt = source[...], target[...]
    for c in range(0, partial.shape[0], CHUNK):
        rows = slice(c, c + CHUNK)
        col = column(src, rows)
        acc = dot(pick(column(tgt, rows), cells), latent)
        partial[rows, :] = acc + dot(pick(col, nodes), own[...])
        picks_out[rows, :] = pick(col - nodes, 2 * nodes)
    spread_out[...] = spread(tgt, cells)
    copy.wait()


def decode_kernel(
    partial, other, mate, picks, spreading, grid, w_update, grid_out, messages
):
    nodes = mate.shape[0]
    for c in range(0, partial.shape[0], CHUNK):
        rows = slice(c, c + CHUNK)
        acc = partial[rows, :] + dot(picks[rows, :nodes], mate[...])
        messages[rows, :] = message(acc + dot(picks[rows, nodes:], other[...]))
    summed = dot(spreading[...], messages[...])
    grid_out[...] = refresh(grid[...], summed, w_update[...])


def on_device(
    grid_latent,
    mesh_latent,
    encode_message,
    encode_update,
    process_message,
    process_update,
    decode_message,
    decode_update,
    encode_source,
    encode_target,
    process_source,
    process_target,
    decode_source,
    decode_target,
):
    lat_rows, lon_cols, width = grid_latent.shape
    bands = lax.axis_size("gx")
    sectors = lax.axis_size("gy")
    sector = lax.axis_index("gy")
    mesh_rows = mesh_latent.reshape(-1, width)
    nodes = mesh_rows.shape[0]
    grid_rows = grid_latent.reshape(-1, width)
    cells = grid_rows.shape[0]
    edges = encode_source.size
    bf16 = jnp.bfloat16
    params = pltpu.CompilerParams(vmem_limit_bytes=40 * 1024 * 1024)
    hbm = pl.BlockSpec(memory_space=pltpu.HBM)
    vmem = pl.BlockSpec(memory_space=pltpu.VMEM)
    assert lon_cols == LON_DEV

    def pinned(array):
        return pltpu.with_memory_space_constraint(array, pltpu.HBM)

    partner = [i + 1 if i % 2 else i - 1 for i in range(max(bands, sectors))]
    far_bands = [(i, partner[i]) for i in range(1, bands - 1)]
    near_bands = [(i, i ^ 1) for i in range(bands)]
    far_sectors = [(i, partner[i] % sectors) for i in range(sectors)]
    near_sectors = [(i, i ^ 1) for i in range(sectors)]

    group = [[i for i in range(sectors) if i // HALF % 2 == h] for h in range(2)]

    every = range(sectors)
    plane_groups = [[i for i in every if i // CORES % HALF == p] for p in range(HALF)]
    columns = [i for i in every if i // CORES % PLANES == 0]
    column_groups = [[i + p * CORES for p in range(PLANES)] for i in columns]

    def exchange(array, groups):
        return lax.all_to_all(array, "gy", 0, 0, axis_index_groups=groups, tiled=True)

    band_edge = jax.ShapeDtypeStruct((lon_cols, width), bf16)
    far, near = pl.pallas_call(
        edges_kernel,
        in_specs=[hbm],
        out_specs=(vmem,) * 2,
        out_shape=(band_edge,) * 2,
        scratch_shapes=[pltpu.SemaphoreType.DMA((2,))],
        compiler_params=params,
    )(pinned(grid_latent))
    far = lax.ppermute(far, "gx", far_bands)
    near = lax.ppermute(near, "gx", near_bands)
    sector_edge = jax.ShapeDtypeStruct((lat_rows + 2, HALO, width), bf16)
    other, mate = pl.pallas_call(
        sides_kernel,
        in_specs=[vmem, hbm, vmem],
        out_specs=(vmem,) * 2,
        out_shape=(sector_edge,) * 2,
        scratch_shapes=[
            pltpu.VMEM((2, lat_rows, HALO, width), bf16),
            pltpu.SemaphoreType.DMA((2,)),
        ],
        compiler_params=params,
    )(far, pinned(grid_latent), near)
    other = lax.ppermute(other, "gy", far_sectors)
    mate = lax.ppermute(mate, "gy", near_sectors)

    tall_cells = (lat_rows + 2) * lon_cols
    depth = -(-2 * (lat_rows + 2) * HALO // LANES) * LANES
    index = jax.ShapeDtypeStruct((edges // LANES, LANES), jnp.int32)
    table_shape = jax.ShapeDtypeStruct((nodes, width), bf16)
    partial_shape = jax.ShapeDtypeStruct((edges, width), jnp.float32)
    spread_shape = jax.ShapeDtypeStruct((nodes, edges), bf16)
    rows_shape = jax.ShapeDtypeStruct((sectors // 2, LANES), jnp.int32)
    plane_shape = jax.ShapeDtypeStruct((sectors // 2 // PLANES, LANES), jnp.int32)
    partial, spreading, mesh_held, weights, sides, slots, order = pl.pallas_call(
        gather_kernel,
        in_specs=[vmem, hbm, vmem] + [hbm] * 8,
        out_specs=(vmem,) * 7,
        out_shape=(
            partial_shape,
            spread_shape,
            table_shape,
            jax.ShapeDtypeStruct((3, width, width), bf16),
            jax.ShapeDtypeStruct((edges, depth), bf16),
            plane_shape,
            index,
        ),
        scratch_shapes=[
            pltpu.VMEM((lat_rows, lon_cols, width), bf16),
            pltpu.VMEM((4, edges // LANES, LANES), jnp.int32),
            pltpu.VMEM(rows_shape.shape, jnp.int32),
            pltpu.VMEM((tall_cells, width), bf16),
            pltpu.SemaphoreType.DMA((9,)),
        ],
        compiler_params=params,
    )(
        far, pinned(grid_latent), near, pinned(mesh_rows), pinned(encode_message),
        pinned(encode_update), pinned(process_message),
        *(
            pinned(array.reshape(-1, LANES))
            for array in (encode_source, encode_target, process_source, process_target)
        ),
    )
    messages = pltpu.VMEM((edges, width), bf16)
    first, following = pl.pallas_call(
        encode_kernel,
        out_shape=(table_shape, table_shape),
        scratch_shapes=[pltpu.VMEM((depth, width), bf16), messages],
        compiler_params=params,
    )(partial, other, mate, spreading, mesh_held, weights, sides)

    following, slots = lax.optimization_barrier((following, slots))
    mirror = lax.ppermute(following, "gy", [(i, i ^ HALF) for i in range(sectors)])
    slots = exchange(slots, plane_groups)
    slots = pl.pallas_call(planes_kernel, out_shape=rows_shape, compiler_params=params)(slots)
    slots = exchange(slots, column_groups)
    send = pl.pallas_call(
        request_kernel,
        out_shape=jax.ShapeDtypeStruct((edges, width), bf16),
        scratch_shapes=[pltpu.VMEM(rows_shape.shape, jnp.int32)],
        compiler_params=params,
    )(following, mirror, slots)
    picked = exchange(send.reshape(sectors // 2, -1, width), group).reshape(edges, width)
    second, table = pl.pallas_call(
        process_kernel,
        out_specs=(hbm, vmem),
        out_shape=(table_shape, table_shape),
        scratch_shapes=[
            messages, pltpu.VMEM((nodes, width), bf16), pltpu.SemaphoreType.DMA(())
        ],
        compiler_params=params,
    )(picked, order, first, process_update, decode_message)

    other = lax.ppermute(table, "gy", far_sectors)
    mate = lax.ppermute(table, "gy", near_sectors)
    source = decode_source.reshape(-1, LANES)
    owner = source // nodes % sectors
    piece = jnp.where(owner == sector, 0, jnp.where(owner == sector ^ 1, 1, 2))
    row = piece * nodes + source % nodes
    target = decode_target.reshape(-1, LANES)
    partial, picks, spreading, update = pl.pallas_call(
        reach_kernel,
        in_specs=[vmem] * 4 + [hbm],
        out_specs=(vmem,) * 4,
        out_shape=(
            partial_shape,
            jax.ShapeDtypeStruct((edges, 2 * nodes), bf16),
            jax.ShapeDtypeStruct((cells, edges), bf16),
            jax.ShapeDtypeStruct((width, width), bf16),
        ),
        scratch_shapes=[pltpu.SemaphoreType.DMA(())],
        compiler_params=params,
    )(table, grid_rows, row, target, pinned(decode_update))
    grid_output = pl.pallas_call(
        decode_kernel,
        out_shape=jax.ShapeDtypeStruct((cells, width), bf16),
        scratch_shapes=[messages],
        compiler_params=params,
    )(partial, other, mate, picks, spreading, grid_rows, update)
    return (
        grid_output.reshape(lat_rows, lon_cols, width),
        second.reshape(1, 1, nodes, width),
    )


def solution(mesh):
    edge = P("gx", "gy", None)
    return jax.shard_map(
        on_device,
        mesh=mesh,
        in_specs=(
            P("gx", "gy", None),
            P("gx", "gy", None, None),
            *([P()] * 6),
            *([edge] * 6),
        ),
        out_specs=(P("gx", "gy", None), P("gx", "gy", None, None)),
        check_vma=False,
    )
```

```python
import jax
import jax.numpy as jnp
from jax import lax
from jax.experimental import pallas as pl
from jax.experimental.pallas import tpu as pltpu
from jax.sharding import PartitionSpec as P

HALO = 8
LON_DEV = 64
EPSILON = 1e-05
LANES = 128
CHUNK = 256
CAP = 16
GROUPS = LANES // CAP
HALF = 8
CORES = 2
PLANES = HALF // CORES


def column(index, rows):
    parts = []
    for i in range(rows.start // LANES, rows.stop // LANES):
        row = jnp.broadcast_to(index[i : i + 1, :], (LANES, LANES))
        parts.append(row.T)
    return jnp.concatenate(parts, axis=0)


def pick(col, count):
    lane = lax.broadcasted_iota(jnp.int32, col.shape, 1)
    parts = [
        jnp.where(col == lane + k, 1.0, 0.0).astype(jnp.bfloat16)
        for k in range(0, count, LANES)
    ]
    return jnp.concatenate(parts, axis=1)


def spread(index, count):
    sub = lax.broadcasted_iota(jnp.int32, (count, LANES), 0)
    parts = [
        jnp.where(index[i : i + 1, :] == sub, 1.0, 0.0).astype(jnp.bfloat16)
        for i in range(index.shape[0])
    ]
    return jnp.concatenate(parts, axis=1)


def dot(a, b):
    return jnp.dot(a, b, preferred_element_type=jnp.float32)


def message(summed):
    half = 0.5 * summed
    return (half * jnp.tanh(half) + half).astype(jnp.bfloat16)


def refresh(latent, summed, weight):
    scaled = summed * lax.rsqrt(jnp.mean(summed * summed, axis=-1, keepdims=True) + EPSILON)
    return (latent.astype(jnp.float32) + dot(scaled.astype(jnp.bfloat16), weight)).astype(
        jnp.bfloat16
    )


def log2(value):
    assert value & (value - 1) == 0
    return value.bit_length() - 1


def roll(value, shift):
    return pltpu.roll(value, shift % LANES, 1) if shift % LANES else value


def apart(slots, out):
    upper = lax.rem(lax.axis_index("gy") // HALF, 2) == 1
    lane = lax.broadcasted_iota(jnp.int32, (1, LANES), 1)
    whole = slots[...]
    for g in range(GROUPS):
        first = roll(whole, -g * CAP)
        second = roll(whole, CAP - g * CAP)
        for y in range(whole.shape[0] // 2):
            low, high = slice(2 * y, 2 * y + 1), slice(2 * y + 1, 2 * y + 2)
            own = jnp.where(upper, first[high], first[low])
            mirror = jnp.where(upper, second[low], second[high])
            at = y * GROUPS + g
            out[at : at + 1, :] = jnp.where(lane < CAP, own, mirror)


def weave(rows, lines, out):
    lane = lax.broadcasted_iota(jnp.int32, (1, LANES), 1)
    each = 2 * CAP
    moved = [roll(rows, g * each) for g in range(LANES // each)]
    for i, line in enumerate(lines):
        kept = moved[0][line[0] : line[0] + 1]
        for g in range(1, len(line)):
            kept = jnp.where(lane >= g * each, moved[g][line[g] : line[g] + 1], kept)
        out[i : i + 1, :] = kept


def in_order(count):
    fold = LANES // (2 * CAP)
    return [[i + g for g in range(fold)] for i in range(0, count, fold)]


def plane_first(rows, count):
    def place(i):
        y, p, core = i // HALF, i % HALF // CORES, i % CORES
        return p * (count // PLANES) + y * CORES + core

    return [[place(i) for i in line] for line in rows]


def beside(count):
    return [
        [y * HALF + p * CORES + core for p in range(PLANES)]
        for y in range(count // HALF)
        for core in range(CORES)
    ]


def planes_kernel(slots, slots_out):
    count = slots.shape[0]
    for p in range(PLANES):
        slots_out[p * count : (p + 1) * count, :] = roll(slots[...], -p * 2 * CAP)


def edges_kernel(grid, far_out, near_out, sems):
    even = lax.rem(lax.axis_index("gx"), 2) == 0
    last = grid.shape[0] - 1
    near = pltpu.make_async_copy(grid.at[jnp.where(even, last, 0)], near_out, sems.at[0])
    far = pltpu.make_async_copy(grid.at[jnp.where(even, 0, last)], far_out, sems.at[1])
    near.start()
    far.start()
    near.wait()
    far.wait()


def sides_kernel(far, grid, near, far_out, near_out, held, sems):
    even = lax.rem(lax.axis_index("gy"), 2) == 0
    lats, lons, _ = grid.shape
    west = pltpu.make_async_copy(grid.at[:, :HALO], held.at[0], sems.at[0])
    east = pltpu.make_async_copy(grid.at[:, lons - HALO :], held.at[1], sems.at[1])
    west.start()
    east.start()
    west.wait()
    east.wait()

    def put(out, side):
        out[0] = near[side, :]
        for i in range(lats):
            out[i + 1] = held[0 if side.start == 0 else 1, i]
        out[lats + 1] = far[side, :]

    first, last = slice(0, HALO), slice(lons - HALO, lons)

    @pl.when(even)
    def _():
        put(near_out, last)
        put(far_out, first)

    @pl.when(jnp.logical_not(even))
    def _():
        put(near_out, first)
        put(far_out, last)


def places(source, lats, lons):
    band, sector = lax.axis_index("gx"), lax.axis_index("gy")
    lon_total = lons * lax.axis_size("gy")
    lat = (source >> log2(lon_total)) - band * lats + 1
    outer = (lat == 0) | (lat == lats + 1)
    lat = jnp.where(outer & (lax.rem(band, 2) == 0), lats + 1 - lat, lat)
    lon = ((source & (lon_total - 1)) - sector * lons + HALO) & (lon_total - 1)
    inner = (lon >= HALO) & (lon < HALO + lons)
    return lat, lon, inner


def gather_kernel(
    far, grid, near, mesh, w_message, w_update, w_next, source, target, next_source, next_target,
    partial, spread_out, mesh_out, w_out, sides_out, slots_out, order_out,
    held, indices, rows_held, table, sems,
):
    pairs = [(source, indices.at[0]), (target, indices.at[1])]
    pairs += [(grid, held), (w_message, w_out.at[0]), (mesh, mesh_out)]
    pairs += [(next_source, indices.at[2]), (next_target, indices.at[3])]
    pairs += [(w_update, w_out.at[1]), (w_next, w_out.at[2])]
    copies = [pltpu.make_async_copy(a, b, sems.at[i]) for i, (a, b) in enumerate(pairs)]
    for copy in copies:
        copy.start()
    lats, lons, width = grid.shape
    nodes = mesh.shape[0]
    copies[0].wait()
    copies[1].wait()
    lat, lon, inner = places(indices[0], lats, lons)
    src = jnp.where(inner, lat * lons + lon - HALO, -1)
    tgt = indices[1]
    edges = src.shape[0] * LANES
    spread_out[...] = spread(tgt, nodes)
    copies[2].wait()
    copies[3].wait()
    w = w_out[0]
    table[:lons, :] = dot(near[...], w).astype(jnp.bfloat16)
    inside = held[...].reshape(lats * lons, width)
    table[lons : (lats + 1) * lons, :] = dot(inside, w).astype(jnp.bfloat16)
    table[(lats + 1) * lons :, :] = dot(far[...], w).astype(jnp.bfloat16)
    copies[4].wait()
    depth = table.shape[0]
    side = (lats + 2) * HALO
    on_mate = (lon >= HALO) == (lax.rem(lax.axis_index("gy"), 2) == 0)
    edge = jnp.where(on_mate, 0, side) + lat * HALO + (lon & (HALO - 1))
    edge = jnp.where(inner, -1, edge)
    for c in range(0, edges, CHUNK):
        rows = slice(c, c + CHUNK)
        acc = dot(pick(column(src, rows), depth), table[...])
        partial[rows, :] = acc + dot(pick(column(tgt, rows), nodes), mesh_out[...])
        sides_out[rows, :] = pick(column(edge, rows), sides_out.shape[1])
    copies[5].wait()
    copies[6].wait()
    apart(indices.at[2], rows_held)
    weave(rows_held[...], beside(rows_held.shape[0]), slots_out)
    apart(indices.at[3], rows_held)
    weave(rows_held[...], in_order(rows_held.shape[0]), order_out)
    copies[7].wait()
    copies[8].wait()


def encode_kernel(
    partial, other, mate, spreading, mesh, weights, sides,
    first_out, next_out, table, messages,
):
    w = weights[0]
    tall, halo, width = mate.shape
    side = tall * halo
    table[:side, :] = dot(mate[...].reshape(side, width), w).astype(jnp.bfloat16)
    table[side : 2 * side, :] = dot(other[...].reshape(side, width), w).astype(jnp.bfloat16)
    table[2 * side :, :] = jnp.zeros((table.shape[0] - 2 * side, width), jnp.bfloat16)
    edges = partial.shape[0]
    for c in range(0, edges, CHUNK):
        rows = slice(c, c + CHUNK)
        messages[rows, :] = message(partial[rows, :] + dot(sides[rows, :], table[...]))
    summed = dot(spreading[...], messages[...])
    first = refresh(mesh[...], summed, weights[1])
    first_out[...] = first
    next_out[...] = dot(first, weights[2]).astype(jnp.bfloat16)


def request_kernel(table, mirror, slots, send_out, held):
    nodes = table.shape[0]
    count = slots.shape[0]
    weave(slots[...], plane_first(in_order(count), count), held)
    asked = held[...]
    lane = lax.broadcasted_iota(jnp.int32, asked.shape, 1)
    asked = asked + jnp.where((lane & (2 * CAP - 1)) >= CAP, nodes, 0)
    for c in range(0, send_out.shape[0], CHUNK):
        rows = slice(c, c + CHUNK)
        col = column(asked, rows)
        acc = dot(pick(col, nodes), table[...]) + dot(pick(col - nodes, nodes), mirror[...])
        send_out[rows, :] = acc.astype(jnp.bfloat16)


def process_kernel(
    picked, target, first, w_update, w_next, second_out, table_out, messages, held, sem
):
    nodes = first.shape[0]
    tgt = target[...]
    for c in range(0, picked.shape[0], CHUNK):
        rows = slice(c, c + CHUNK)
        acc = dot(pick(column(tgt, rows), nodes), first[...])
        messages[rows, :] = message(acc + picked[rows, :].astype(jnp.float32))
    second = refresh(first[...], dot(spread(tgt, nodes), messages[...]), w_update[...])
    held[...] = second
    copy = pltpu.make_async_copy(held, second_out, sem)
    copy.start()
    table_out[...] = dot(second, w_next[...]).astype(jnp.bfloat16)
    copy.wait()


def reach_kernel(
    own, grid, source, target, w_update, partial, picks_out, spread_out, w_out, sem
):
    copy = pltpu.make_async_copy(w_update, w_out, sem)
    copy.start()
    latent = grid[...]
    cells = latent.shape[0]
    nodes = own.shape[0]
    src, tgt = source[...], target[...]
    for c in range(0, partial.shape[0], CHUNK):
        rows = slice(c, c + CHUNK)
        col = column(src, rows)
        acc = dot(pick(column(tgt, rows), cells), latent)
        partial[rows, :] = acc + dot(pick(col, nodes), own[...])
        picks_out[rows, :] = pick(col - nodes, 2 * nodes)
    spread_out[...] = spread(tgt, cells)
    copy.wait()


def decode_kernel(
    partial, other, mate, picks, spreading, grid, w_update, grid_out, messages
):
    nodes = mate.shape[0]
    for c in range(0, partial.shape[0], CHUNK):
        rows = slice(c, c + CHUNK)
        acc = partial[rows, :] + dot(picks[rows, :nodes], mate[...])
        messages[rows, :] = message(acc + dot(picks[rows, nodes:], other[...]))
    summed = dot(spreading[...], messages[...])
    grid_out[...] = refresh(grid[...], summed, w_update[...])


def on_device(
    grid_latent,
    mesh_latent,
    encode_message,
    encode_update,
    process_message,
    process_update,
    decode_message,
    decode_update,
    encode_source,
    encode_target,
    process_source,
    process_target,
    decode_source,
    decode_target,
):
    lat_rows, lon_cols, width = grid_latent.shape
    bands = lax.axis_size("gx")
    sectors = lax.axis_size("gy")
    sector = lax.axis_index("gy")
    mesh_rows = mesh_latent.reshape(-1, width)
    nodes = mesh_rows.shape[0]
    grid_rows = grid_latent.reshape(-1, width)
    cells = grid_rows.shape[0]
    edges = encode_source.size
    bf16 = jnp.bfloat16
    params = pltpu.CompilerParams(vmem_limit_bytes=40 * 1024 * 1024)
    hbm = pl.BlockSpec(memory_space=pltpu.HBM)
    vmem = pl.BlockSpec(memory_space=pltpu.VMEM)
    assert lon_cols == LON_DEV

    def pinned(array):
        return pltpu.with_memory_space_constraint(array, pltpu.HBM)

    partner = [i + 1 if i % 2 else i - 1 for i in range(max(bands, sectors))]
    far_bands = [(i, partner[i]) for i in range(1, bands - 1)]
    near_bands = [(i, i ^ 1) for i in range(bands)]
    far_sectors = [(i, partner[i] % sectors) for i in range(sectors)]
    near_sectors = [(i, i ^ 1) for i in range(sectors)]

    group = [[i for i in range(sectors) if i // HALF % 2 == h] for h in range(2)]

    every = range(sectors)
    plane_groups = [[i for i in every if i // CORES % HALF == p] for p in range(HALF)]
    columns = [i for i in every if i // CORES % PLANES == 0]
    column_groups = [[i + p * CORES for p in range(PLANES)] for i in columns]

    def exchange(array, groups):
        return lax.all_to_all(array, "gy", 0, 0, axis_index_groups=groups, tiled=True)

    band_edge = jax.ShapeDtypeStruct((lon_cols, width), bf16)
    far, near = pl.pallas_call(
        edges_kernel,
        in_specs=[hbm],
        out_specs=(vmem,) * 2,
        out_shape=(band_edge,) * 2,
        scratch_shapes=[pltpu.SemaphoreType.DMA((2,))],
        compiler_params=params,
    )(pinned(grid_latent))
    far = lax.ppermute(far, "gx", far_bands)
    near = lax.ppermute(near, "gx", near_bands)
    sector_edge = jax.ShapeDtypeStruct((lat_rows + 2, HALO, width), bf16)
    other, mate = pl.pallas_call(
        sides_kernel,
        in_specs=[vmem, hbm, vmem],
        out_specs=(vmem,) * 2,
        out_shape=(sector_edge,) * 2,
        scratch_shapes=[
            pltpu.VMEM((2, lat_rows, HALO, width), bf16),
            pltpu.SemaphoreType.DMA((2,)),
        ],
        compiler_params=params,
    )(far, pinned(grid_latent), near)
    other = lax.ppermute(other, "gy", far_sectors)
    mate = lax.ppermute(mate, "gy", near_sectors)

    tall_cells = (lat_rows + 2) * lon_cols
    depth = -(-2 * (lat_rows + 2) * HALO // LANES) * LANES
    index = jax.ShapeDtypeStruct((edges // LANES, LANES), jnp.int32)
    table_shape = jax.ShapeDtypeStruct((nodes, width), bf16)
    partial_shape = jax.ShapeDtypeStruct((edges, width), jnp.float32)
    spread_shape = jax.ShapeDtypeStruct((nodes, edges), bf16)
    rows_shape = jax.ShapeDtypeStruct((sectors // 2, LANES), jnp.int32)
    plane_shape = jax.ShapeDtypeStruct((sectors // 2 // PLANES, LANES), jnp.int32)
    partial, spreading, mesh_held, weights, sides, slots, order = pl.pallas_call(
        gather_kernel,
        in_specs=[vmem, hbm, vmem] + [hbm] * 8,
        out_specs=(vmem,) * 7,
        out_shape=(
            partial_shape,
            spread_shape,
            table_shape,
            jax.ShapeDtypeStruct((3, width, width), bf16),
            jax.ShapeDtypeStruct((edges, depth), bf16),
            plane_shape,
            index,
        ),
        scratch_shapes=[
            pltpu.VMEM((lat_rows, lon_cols, width), bf16),
            pltpu.VMEM((4, edges // LANES, LANES), jnp.int32),
            pltpu.VMEM(rows_shape.shape, jnp.int32),
            pltpu.VMEM((tall_cells, width), bf16),
            pltpu.SemaphoreType.DMA((9,)),
        ],
        compiler_params=params,
    )(
        far, pinned(grid_latent), near, pinned(mesh_rows), pinned(encode_message),
        pinned(encode_update), pinned(process_message),
        *(
            pinned(array.reshape(-1, LANES))
            for array in (encode_source, encode_target, process_source, process_target)
        ),
    )
    messages = pltpu.VMEM((edges, width), bf16)
    first, following = pl.pallas_call(
        encode_kernel,
        out_shape=(table_shape, table_shape),
        scratch_shapes=[pltpu.VMEM((depth, width), bf16), messages],
        compiler_params=params,
    )(partial, other, mate, spreading, mesh_held, weights, sides)

    following, slots = lax.optimization_barrier((following, slots))
    mirror = lax.ppermute(following, "gy", [(i, i ^ HALF) for i in range(sectors)])
    slots = exchange(slots, plane_groups)
    slots = pl.pallas_call(planes_kernel, out_shape=rows_shape, compiler_params=params)(slots)
    slots = exchange(slots, column_groups)
    send = pl.pallas_call(
        request_kernel,
        out_shape=jax.ShapeDtypeStruct((edges, width), bf16),
        scratch_shapes=[pltpu.VMEM(index.shape, jnp.int32)],
        compiler_params=params,
    )(following, mirror, slots)
    picked = exchange(send.reshape(sectors // 2, -1, width), group).reshape(edges, width)
    second, table = pl.pallas_call(
        process_kernel,
        out_specs=(hbm, vmem),
        out_shape=(table_shape, table_shape),
        scratch_shapes=[
            messages, pltpu.VMEM((nodes, width), bf16), pltpu.SemaphoreType.DMA(())
        ],
        compiler_params=params,
    )(picked, order, first, process_update, decode_message)

    other = lax.ppermute(table, "gy", far_sectors)
    mate = lax.ppermute(table, "gy", near_sectors)
    source = decode_source.reshape(-1, LANES)
    owner = source // nodes % sectors
    piece = jnp.where(owner == sector, 0, jnp.where(owner == sector ^ 1, 1, 2))
    row = piece * nodes + source % nodes
    target = decode_target.reshape(-1, LANES)
    partial, picks, spreading, update = pl.pallas_call(
        reach_kernel,
        in_specs=[vmem] * 4 + [hbm],
        out_specs=(vmem,) * 4,
        out_shape=(
            partial_shape,
            jax.ShapeDtypeStruct((edges, 2 * nodes), bf16),
            jax.ShapeDtypeStruct((cells, edges), bf16),
            jax.ShapeDtypeStruct((width, width), bf16),
        ),
        scratch_shapes=[pltpu.SemaphoreType.DMA(())],
        compiler_params=params,
    )(table, grid_rows, row, target, pinned(decode_update))
    grid_output = pl.pallas_call(
        decode_kernel,
        out_shape=jax.ShapeDtypeStruct((cells, width), bf16),
        scratch_shapes=[messages],
        compiler_params=params,
    )(partial, other, mate, picks, spreading, grid_rows, update)
    return (
        grid_output.reshape(lat_rows, lon_cols, width),
        second.reshape(1, 1, nodes, width),
    )


def solution(mesh):
    edge = P("gx", "gy", None)
    return jax.shard_map(
        on_device,
        mesh=mesh,
        in_specs=(
            P("gx", "gy", None),
            P("gx", "gy", None, None),
            *([P()] * 6),
            *([edge] * 6),
        ),
        out_specs=(P("gx", "gy", None), P("gx", "gy", None, None)),
        check_vma=False,
    )
```

```python
import jax
import jax.numpy as jnp
from jax import lax
from jax.experimental import pallas as pl
from jax.experimental.pallas import tpu as pltpu
from jax.sharding import PartitionSpec as P

HALO = 8
LON_DEV = 64
EPSILON = 1e-05
LANES = 128
CHUNK = 1024
CAP = 16
GROUPS = LANES // CAP
HALF = 8
CORES = 2
PLANES = HALF // CORES


def column(index, rows):
    parts = []
    for i in range(rows.start // LANES, rows.stop // LANES):
        row = jnp.broadcast_to(index[i : i + 1, :], (LANES, LANES))
        parts.append(row.T)
    return jnp.concatenate(parts, axis=0)


def pick(col, count):
    lane = lax.broadcasted_iota(jnp.int32, col.shape, 1)
    parts = [
        jnp.where(col == lane + k, 1.0, 0.0).astype(jnp.bfloat16)
        for k in range(0, count, LANES)
    ]
    return jnp.concatenate(parts, axis=1)


def spread(index, count):
    sub = lax.broadcasted_iota(jnp.int32, (count, LANES), 0)
    parts = [
        jnp.where(index[i : i + 1, :] == sub, 1.0, 0.0).astype(jnp.bfloat16)
        for i in range(index.shape[0])
    ]
    return jnp.concatenate(parts, axis=1)


def dot(a, b):
    return jnp.dot(a, b, preferred_element_type=jnp.float32)


def message(summed):
    half = 0.5 * summed
    return (half * jnp.tanh(half) + half).astype(jnp.bfloat16)


def refresh(latent, summed, weight):
    scaled = summed * lax.rsqrt(jnp.mean(summed * summed, axis=-1, keepdims=True) + EPSILON)
    return (latent.astype(jnp.float32) + dot(scaled.astype(jnp.bfloat16), weight)).astype(
        jnp.bfloat16
    )


def log2(value):
    assert value & (value - 1) == 0
    return value.bit_length() - 1


def roll(value, shift):
    return pltpu.roll(value, shift % LANES, 1) if shift % LANES else value


def apart(slots, out):
    upper = lax.rem(lax.axis_index("gy") // HALF, 2) == 1
    lane = lax.broadcasted_iota(jnp.int32, (1, LANES), 1)
    whole = slots[...]
    for g in range(GROUPS):
        first = roll(whole, -g * CAP)
        second = roll(whole, CAP - g * CAP)
        for y in range(whole.shape[0] // 2):
            low, high = slice(2 * y, 2 * y + 1), slice(2 * y + 1, 2 * y + 2)
            own = jnp.where(upper, first[high], first[low])
            mirror = jnp.where(upper, second[low], second[high])
            at = y * GROUPS + g
            out[at : at + 1, :] = jnp.where(lane < CAP, own, mirror)


def weave(rows, lines, out):
    lane = lax.broadcasted_iota(jnp.int32, (1, LANES), 1)
    each = 2 * CAP
    moved = [roll(rows, g * each) for g in range(LANES // each)]
    for i, line in enumerate(lines):
        kept = moved[0][line[0] : line[0] + 1]
        for g in range(1, len(line)):
            kept = jnp.where(lane >= g * each, moved[g][line[g] : line[g] + 1], kept)
        out[i : i + 1, :] = kept


def in_order(count):
    fold = LANES // (2 * CAP)
    return [[i + g for g in range(fold)] for i in range(0, count, fold)]


def plane_first(rows, count):
    def place(i):
        y, p, core = i // HALF, i % HALF // CORES, i % CORES
        return p * (count // PLANES) + y * CORES + core

    return [[place(i) for i in line] for line in rows]


def beside(count):
    return [
        [y * HALF + p * CORES + core for p in range(PLANES)]
        for y in range(count // HALF)
        for core in range(CORES)
    ]


def planes_kernel(slots, slots_out):
    count = slots.shape[0]
    for p in range(PLANES):
        slots_out[p * count : (p + 1) * count, :] = roll(slots[...], -p * 2 * CAP)


def edges_kernel(grid, far_out, near_out, sems):
    even = lax.rem(lax.axis_index("gx"), 2) == 0
    last = grid.shape[0] - 1
    near = pltpu.make_async_copy(grid.at[jnp.where(even, last, 0)], near_out, sems.at[0])
    far = pltpu.make_async_copy(grid.at[jnp.where(even, 0, last)], far_out, sems.at[1])
    near.start()
    far.start()
    near.wait()
    far.wait()


def sides_kernel(far, grid, near, far_out, near_out, held, sems):
    even = lax.rem(lax.axis_index("gy"), 2) == 0
    lats, lons, _ = grid.shape
    west = pltpu.make_async_copy(grid.at[:, :HALO], held.at[0], sems.at[0])
    east = pltpu.make_async_copy(grid.at[:, lons - HALO :], held.at[1], sems.at[1])
    west.start()
    east.start()
    west.wait()
    east.wait()

    def put(out, side):
        out[0] = near[side, :]
        for i in range(lats):
            out[i + 1] = held[0 if side.start == 0 else 1, i]
        out[lats + 1] = far[side, :]

    first, last = slice(0, HALO), slice(lons - HALO, lons)

    @pl.when(even)
    def _():
        put(near_out, last)
        put(far_out, first)

    @pl.when(jnp.logical_not(even))
    def _():
        put(near_out, first)
        put(far_out, last)


def places(source, lats, lons):
    band, sector = lax.axis_index("gx"), lax.axis_index("gy")
    lon_total = lons * lax.axis_size("gy")
    lat = (source >> log2(lon_total)) - band * lats + 1
    outer = (lat == 0) | (lat == lats + 1)
    lat = jnp.where(outer & (lax.rem(band, 2) == 0), lats + 1 - lat, lat)
    lon = ((source & (lon_total - 1)) - sector * lons + HALO) & (lon_total - 1)
    inner = (lon >= HALO) & (lon < HALO + lons)
    return lat, lon, inner


def gather_kernel(
    far, grid, near, mesh, w_message, w_update, w_next, source, target, next_source, next_target,
    partial, spread_out, mesh_out, w_out, sides_out, slots_out, order_out,
    held, indices, rows_held, table, sems,
):
    pairs = [(source, indices.at[0]), (target, indices.at[1])]
    pairs += [(grid, held), (w_message, w_out.at[0]), (mesh, mesh_out)]
    pairs += [(next_source, indices.at[2]), (next_target, indices.at[3])]
    pairs += [(w_update, w_out.at[1]), (w_next, w_out.at[2])]
    copies = [pltpu.make_async_copy(a, b, sems.at[i]) for i, (a, b) in enumerate(pairs)]
    for copy in copies:
        copy.start()
    lats, lons, width = grid.shape
    nodes = mesh.shape[0]
    copies[0].wait()
    copies[1].wait()
    lat, lon, inner = places(indices[0], lats, lons)
    src = jnp.where(inner, lat * lons + lon - HALO, -1)
    tgt = indices[1]
    edges = src.shape[0] * LANES
    spread_out[...] = spread(tgt, nodes)
    copies[2].wait()
    copies[3].wait()
    w = w_out[0]
    table[:lons, :] = dot(near[...], w).astype(jnp.bfloat16)
    inside = held[...].reshape(lats * lons, width)
    table[lons : (lats + 1) * lons, :] = dot(inside, w).astype(jnp.bfloat16)
    table[(lats + 1) * lons :, :] = dot(far[...], w).astype(jnp.bfloat16)
    copies[4].wait()
    depth = table.shape[0]
    side = (lats + 2) * HALO
    on_mate = (lon >= HALO) == (lax.rem(lax.axis_index("gy"), 2) == 0)
    edge = jnp.where(on_mate, 0, side) + lat * HALO + (lon & (HALO - 1))
    edge = jnp.where(inner, -1, edge)
    for c in range(0, edges, CHUNK):
        rows = slice(c, c + CHUNK)
        acc = dot(pick(column(src, rows), depth), table[...])
        partial[rows, :] = acc + dot(pick(column(tgt, rows), nodes), mesh_out[...])
        sides_out[rows, :] = pick(column(edge, rows), sides_out.shape[1])
    copies[5].wait()
    copies[6].wait()
    apart(indices.at[2], rows_held)
    weave(rows_held[...], beside(rows_held.shape[0]), slots_out)
    apart(indices.at[3], rows_held)
    weave(rows_held[...], in_order(rows_held.shape[0]), order_out)
    copies[7].wait()
    copies[8].wait()


def encode_kernel(
    partial, other, mate, spreading, mesh, weights, sides,
    first_out, next_out, table, messages,
):
    w = weights[0]
    tall, halo, width = mate.shape
    side = tall * halo
    table[:side, :] = dot(mate[...].reshape(side, width), w).astype(jnp.bfloat16)
    table[side : 2 * side, :] = dot(other[...].reshape(side, width), w).astype(jnp.bfloat16)
    table[2 * side :, :] = jnp.zeros((table.shape[0] - 2 * side, width), jnp.bfloat16)
    edges = partial.shape[0]
    for c in range(0, edges, CHUNK):
        rows = slice(c, c + CHUNK)
        messages[rows, :] = message(partial[rows, :] + dot(sides[rows, :], table[...]))
    summed = dot(spreading[...], messages[...])
    first = refresh(mesh[...], summed, weights[1])
    first_out[...] = first
    next_out[...] = dot(first, weights[2]).astype(jnp.bfloat16)


def request_kernel(table, mirror, slots, send_out, held):
    nodes = table.shape[0]
    count = slots.shape[0]
    weave(slots[...], plane_first(in_order(count), count), held)
    asked = held[...]
    lane = lax.broadcasted_iota(jnp.int32, asked.shape, 1)
    asked = asked + jnp.where((lane & (2 * CAP - 1)) >= CAP, nodes, 0)
    for c in range(0, send_out.shape[0], CHUNK):
        rows = slice(c, c + CHUNK)
        col = column(asked, rows)
        acc = dot(pick(col, nodes), table[...]) + dot(pick(col - nodes, nodes), mirror[...])
        send_out[rows, :] = acc.astype(jnp.bfloat16)


def process_kernel(
    picked, target, first, w_update, w_next, second_out, table_out, messages, held, sem
):
    nodes = first.shape[0]
    tgt = target[...]
    for c in range(0, picked.shape[0], CHUNK):
        rows = slice(c, c + CHUNK)
        acc = dot(pick(column(tgt, rows), nodes), first[...])
        messages[rows, :] = message(acc + picked[rows, :].astype(jnp.float32))
    second = refresh(first[...], dot(spread(tgt, nodes), messages[...]), w_update[...])
    held[...] = second
    copy = pltpu.make_async_copy(held, second_out, sem)
    copy.start()
    table_out[...] = dot(second, w_next[...]).astype(jnp.bfloat16)
    copy.wait()


def reach_kernel(
    own, grid, source, target, w_update, partial, picks_out, spread_out, w_out, sem
):
    copy = pltpu.make_async_copy(w_update, w_out, sem)
    copy.start()
    latent = grid[...]
    cells = latent.shape[0]
    nodes = own.shape[0]
    src, tgt = source[...], target[...]
    for c in range(0, partial.shape[0], CHUNK):
        rows = slice(c, c + CHUNK)
        col = column(src, rows)
        acc = dot(pick(column(tgt, rows), cells), latent)
        partial[rows, :] = acc + dot(pick(col, nodes), own[...])
        picks_out[rows, :] = pick(col - nodes, 2 * nodes)
    spread_out[...] = spread(tgt, cells)
    copy.wait()


def decode_kernel(
    partial, other, mate, picks, spreading, grid, w_update, grid_out, messages
):
    nodes = mate.shape[0]
    for c in range(0, partial.shape[0], CHUNK):
        rows = slice(c, c + CHUNK)
        acc = partial[rows, :] + dot(picks[rows, :nodes], mate[...])
        messages[rows, :] = message(acc + dot(picks[rows, nodes:], other[...]))
    summed = dot(spreading[...], messages[...])
    grid_out[...] = refresh(grid[...], summed, w_update[...])


def on_device(
    grid_latent,
    mesh_latent,
    encode_message,
    encode_update,
    process_message,
    process_update,
    decode_message,
    decode_update,
    encode_source,
    encode_target,
    process_source,
    process_target,
    decode_source,
    decode_target,
):
    lat_rows, lon_cols, width = grid_latent.shape
    bands = lax.axis_size("gx")
    sectors = lax.axis_size("gy")
    sector = lax.axis_index("gy")
    mesh_rows = mesh_latent.reshape(-1, width)
    nodes = mesh_rows.shape[0]
    grid_rows = grid_latent.reshape(-1, width)
    cells = grid_rows.shape[0]
    edges = encode_source.size
    bf16 = jnp.bfloat16
    params = pltpu.CompilerParams(vmem_limit_bytes=40 * 1024 * 1024)
    hbm = pl.BlockSpec(memory_space=pltpu.HBM)
    vmem = pl.BlockSpec(memory_space=pltpu.VMEM)
    assert lon_cols == LON_DEV

    def pinned(array):
        return pltpu.with_memory_space_constraint(array, pltpu.HBM)

    partner = [i + 1 if i % 2 else i - 1 for i in range(max(bands, sectors))]
    far_bands = [(i, partner[i]) for i in range(1, bands - 1)]
    near_bands = [(i, i ^ 1) for i in range(bands)]
    far_sectors = [(i, partner[i] % sectors) for i in range(sectors)]
    near_sectors = [(i, i ^ 1) for i in range(sectors)]

    group = [[i for i in range(sectors) if i // HALF % 2 == h] for h in range(2)]

    every = range(sectors)
    plane_groups = [[i for i in every if i // CORES % HALF == p] for p in range(HALF)]
    columns = [i for i in every if i // CORES % PLANES == 0]
    column_groups = [[i + p * CORES for p in range(PLANES)] for i in columns]

    def exchange(array, groups):
        return lax.all_to_all(array, "gy", 0, 0, axis_index_groups=groups, tiled=True)

    band_edge = jax.ShapeDtypeStruct((lon_cols, width), bf16)
    far, near = pl.pallas_call(
        edges_kernel,
        in_specs=[hbm],
        out_specs=(vmem,) * 2,
        out_shape=(band_edge,) * 2,
        scratch_shapes=[pltpu.SemaphoreType.DMA((2,))],
        compiler_params=params,
    )(pinned(grid_latent))
    far = lax.ppermute(far, "gx", far_bands)
    near = lax.ppermute(near, "gx", near_bands)
    sector_edge = jax.ShapeDtypeStruct((lat_rows + 2, HALO, width), bf16)
    other, mate = pl.pallas_call(
        sides_kernel,
        in_specs=[vmem, hbm, vmem],
        out_specs=(vmem,) * 2,
        out_shape=(sector_edge,) * 2,
        scratch_shapes=[
            pltpu.VMEM((2, lat_rows, HALO, width), bf16),
            pltpu.SemaphoreType.DMA((2,)),
        ],
        compiler_params=params,
    )(far, pinned(grid_latent), near)
    other = lax.ppermute(other, "gy", far_sectors)
    mate = lax.ppermute(mate, "gy", near_sectors)

    tall_cells = (lat_rows + 2) * lon_cols
    depth = -(-2 * (lat_rows + 2) * HALO // LANES) * LANES
    index = jax.ShapeDtypeStruct((edges // LANES, LANES), jnp.int32)
    table_shape = jax.ShapeDtypeStruct((nodes, width), bf16)
    partial_shape = jax.ShapeDtypeStruct((edges, width), jnp.float32)
    spread_shape = jax.ShapeDtypeStruct((nodes, edges), bf16)
    rows_shape = jax.ShapeDtypeStruct((sectors // 2, LANES), jnp.int32)
    plane_shape = jax.ShapeDtypeStruct((sectors // 2 // PLANES, LANES), jnp.int32)
    partial, spreading, mesh_held, weights, sides, slots, order = pl.pallas_call(
        gather_kernel,
        in_specs=[vmem, hbm, vmem] + [hbm] * 8,
        out_specs=(vmem,) * 7,
        out_shape=(
            partial_shape,
            spread_shape,
            table_shape,
            jax.ShapeDtypeStruct((3, width, width), bf16),
            jax.ShapeDtypeStruct((edges, depth), bf16),
            plane_shape,
            index,
        ),
        scratch_shapes=[
            pltpu.VMEM((lat_rows, lon_cols, width), bf16),
            pltpu.VMEM((4, edges // LANES, LANES), jnp.int32),
            pltpu.VMEM(rows_shape.shape, jnp.int32),
            pltpu.VMEM((tall_cells, width), bf16),
            pltpu.SemaphoreType.DMA((9,)),
        ],
        compiler_params=params,
    )(
        far, pinned(grid_latent), near, pinned(mesh_rows), pinned(encode_message),
        pinned(encode_update), pinned(process_message),
        *(
            pinned(array.reshape(-1, LANES))
            for array in (encode_source, encode_target, process_source, process_target)
        ),
    )
    messages = pltpu.VMEM((edges, width), bf16)
    first, following = pl.pallas_call(
        encode_kernel,
        out_shape=(table_shape, table_shape),
        scratch_shapes=[pltpu.VMEM((depth, width), bf16), messages],
        compiler_params=params,
    )(partial, other, mate, spreading, mesh_held, weights, sides)

    following, slots = lax.optimization_barrier((following, slots))
    mirror = lax.ppermute(following, "gy", [(i, i ^ HALF) for i in range(sectors)])
    slots = exchange(slots, plane_groups)
    slots = pl.pallas_call(planes_kernel, out_shape=rows_shape, compiler_params=params)(slots)
    slots = exchange(slots, column_groups)
    send = pl.pallas_call(
        request_kernel,
        out_shape=jax.ShapeDtypeStruct((edges, width), bf16),
        scratch_shapes=[pltpu.VMEM(index.shape, jnp.int32)],
        compiler_params=params,
    )(following, mirror, slots)
    picked = exchange(send.reshape(sectors // 2, -1, width), group).reshape(edges, width)
    second, table = pl.pallas_call(
        process_kernel,
        out_specs=(hbm, vmem),
        out_shape=(table_shape, table_shape),
        scratch_shapes=[
            messages, pltpu.VMEM((nodes, width), bf16), pltpu.SemaphoreType.DMA(())
        ],
        compiler_params=params,
    )(picked, order, first, process_update, decode_message)

    other = lax.ppermute(table, "gy", far_sectors)
    mate = lax.ppermute(table, "gy", near_sectors)
    source = decode_source.reshape(-1, LANES)
    owner = source // nodes % sectors
    piece = jnp.where(owner == sector, 0, jnp.where(owner == sector ^ 1, 1, 2))
    row = piece * nodes + source % nodes
    target = decode_target.reshape(-1, LANES)
    partial, picks, spreading, update = pl.pallas_call(
        reach_kernel,
        in_specs=[vmem] * 4 + [hbm],
        out_specs=(vmem,) * 4,
        out_shape=(
            partial_shape,
            jax.ShapeDtypeStruct((edges, 2 * nodes), bf16),
            jax.ShapeDtypeStruct((cells, edges), bf16),
            jax.ShapeDtypeStruct((width, width), bf16),
        ),
        scratch_shapes=[pltpu.SemaphoreType.DMA(())],
        compiler_params=params,
    )(table, grid_rows, row, target, pinned(decode_update))
    grid_output = pl.pallas_call(
        decode_kernel,
        out_shape=jax.ShapeDtypeStruct((cells, width), bf16),
        scratch_shapes=[messages],
        compiler_params=params,
    )(partial, other, mate, picks, spreading, grid_rows, update)
    return (
        grid_output.reshape(lat_rows, lon_cols, width),
        second.reshape(1, 1, nodes, width),
    )


def solution(mesh):
    edge = P("gx", "gy", None)
    return jax.shard_map(
        on_device,
        mesh=mesh,
        in_specs=(
            P("gx", "gy", None),
            P("gx", "gy", None, None),
            *([P()] * 6),
            *([edge] * 6),
        ),
        out_specs=(P("gx", "gy", None), P("gx", "gy", None, None)),
        check_vma=False,
    )
```

```python
import jax
import jax.numpy as jnp
from jax import lax
from jax.experimental import pallas as pl
from jax.experimental.pallas import tpu as pltpu
from jax.sharding import PartitionSpec as P

HALO = 8
LON_DEV = 64
EPSILON = 1e-05
LANES = 128
CHUNK = 256
CAP = 16
GROUPS = LANES // CAP
HALF = 8
CORES = 2
PLANES = HALF // CORES


def column(index, rows):
    parts = []
    for i in range(rows.start // LANES, rows.stop // LANES):
        row = jnp.broadcast_to(index[i : i + 1, :], (LANES, LANES))
        parts.append(row.T)
    return jnp.concatenate(parts, axis=0)


def pick(col, count):
    lane = lax.broadcasted_iota(jnp.int32, col.shape, 1)
    parts = [
        jnp.where(col == lane + k, 1.0, 0.0).astype(jnp.bfloat16)
        for k in range(0, count, LANES)
    ]
    return jnp.concatenate(parts, axis=1)


def spread(index, count):
    sub = lax.broadcasted_iota(jnp.int32, (count, LANES), 0)
    parts = [
        jnp.where(index[i : i + 1, :] == sub, 1.0, 0.0).astype(jnp.bfloat16)
        for i in range(index.shape[0])
    ]
    return jnp.concatenate(parts, axis=1)


def dot(a, b):
    return jnp.dot(a, b, preferred_element_type=jnp.float32)


def message(summed):
    half = 0.5 * summed
    return (half * jnp.tanh(half) + half).astype(jnp.bfloat16)


def refresh(latent, summed, weight):
    scaled = summed * lax.rsqrt(jnp.mean(summed * summed, axis=-1, keepdims=True) + EPSILON)
    return (latent.astype(jnp.float32) + dot(scaled.astype(jnp.bfloat16), weight)).astype(
        jnp.bfloat16
    )


def log2(value):
    assert value & (value - 1) == 0
    return value.bit_length() - 1


def roll(value, shift):
    return pltpu.roll(value, shift % LANES, 1) if shift % LANES else value


def apart(slots, out):
    upper = lax.rem(lax.axis_index("gy") // HALF, 2) == 1
    lane = lax.broadcasted_iota(jnp.int32, (1, LANES), 1)
    whole = slots[...]
    for g in range(GROUPS):
        first = roll(whole, -g * CAP)
        second = roll(whole, CAP - g * CAP)
        for y in range(whole.shape[0] // 2):
            low, high = slice(2 * y, 2 * y + 1), slice(2 * y + 1, 2 * y + 2)
            own = jnp.where(upper, first[high], first[low])
            mirror = jnp.where(upper, second[low], second[high])
            at = y * GROUPS + g
            out[at : at + 1, :] = jnp.where(lane < CAP, own, mirror)


def weave(rows, lines, out):
    lane = lax.broadcasted_iota(jnp.int32, (1, LANES), 1)
    each = 2 * CAP
    moved = [roll(rows, g * each) for g in range(LANES // each)]
    for i, line in enumerate(lines):
        kept = moved[0][line[0] : line[0] + 1]
        for g in range(1, len(line)):
            kept = jnp.where(lane >= g * each, moved[g][line[g] : line[g] + 1], kept)
        out[i : i + 1, :] = kept


def in_order(count):
    fold = LANES // (2 * CAP)
    return [[i + g for g in range(fold)] for i in range(0, count, fold)]


def plane_first(rows, count):
    def place(i):
        y, p, core = i // HALF, i % HALF // CORES, i % CORES
        return p * (count // PLANES) + y * CORES + core

    return [[place(i) for i in line] for line in rows]


def beside(count):
    return [
        [y * HALF + p * CORES + core for p in range(PLANES)]
        for y in range(count // HALF)
        for core in range(CORES)
    ]


def planes_kernel(slots, slots_out):
    count = slots.shape[0]
    for p in range(PLANES):
        slots_out[p * count : (p + 1) * count, :] = roll(slots[...], -p * 2 * CAP)


def edges_kernel(grid, far_out, near_out, sems):
    even = lax.rem(lax.axis_index("gx"), 2) == 0
    last = grid.shape[0] - 1
    near = pltpu.make_async_copy(grid.at[jnp.where(even, last, 0)], near_out, sems.at[0])
    far = pltpu.make_async_copy(grid.at[jnp.where(even, 0, last)], far_out, sems.at[1])
    near.start()
    far.start()
    near.wait()
    far.wait()


def sides_kernel(far, grid, near, far_out, near_out, held, sems):
    even = lax.rem(lax.axis_index("gy"), 2) == 0
    lats, lons, _ = grid.shape
    west = pltpu.make_async_copy(grid.at[:, :HALO], held.at[0], sems.at[0])
    east = pltpu.make_async_copy(grid.at[:, lons - HALO :], held.at[1], sems.at[1])
    west.start()
    east.start()
    west.wait()
    east.wait()

    def put(out, side):
        out[0] = near[side, :]
        for i in range(lats):
            out[i + 1] = held[0 if side.start == 0 else 1, i]
        out[lats + 1] = far[side, :]

    first, last = slice(0, HALO), slice(lons - HALO, lons)

    @pl.when(even)
    def _():
        put(near_out, last)
        put(far_out, first)

    @pl.when(jnp.logical_not(even))
    def _():
        put(near_out, first)
        put(far_out, last)


def places(source, lats, lons):
    band, sector = lax.axis_index("gx"), lax.axis_index("gy")
    lon_total = lons * lax.axis_size("gy")
    lat = (source >> log2(lon_total)) - band * lats + 1
    outer = (lat == 0) | (lat == lats + 1)
    lat = jnp.where(outer & (lax.rem(band, 2) == 0), lats + 1 - lat, lat)
    lon = ((source & (lon_total - 1)) - sector * lons + HALO) & (lon_total - 1)
    inner = (lon >= HALO) & (lon < HALO + lons)
    return lat, lon, inner


def gather_kernel(
    far, grid, near, mesh, w_message, w_update, w_next, source, target, next_source, next_target,
    partial, spread_out, mesh_out, w_out, sides_out, slots_out, order_out,
    held, indices, rows_held, table, sems,
):
    pairs = [(source, indices.at[0]), (target, indices.at[1])]
    pairs += [(grid, held), (w_message, w_out.at[0]), (mesh, mesh_out)]
    pairs += [(next_source, indices.at[2]), (next_target, indices.at[3])]
    pairs += [(w_update, w_out.at[1]), (w_next, w_out.at[2])]
    copies = [pltpu.make_async_copy(a, b, sems.at[i]) for i, (a, b) in enumerate(pairs)]
    for copy in copies:
        copy.start()
    lats, lons, width = grid.shape
    nodes = mesh.shape[0]
    copies[0].wait()
    copies[1].wait()
    lat, lon, inner = places(indices[0], lats, lons)
    src = jnp.where(inner, lat * lons + lon - HALO, -1)
    tgt = indices[1]
    edges = src.shape[0] * LANES
    spread_out[...] = spread(tgt, nodes)
    copies[2].wait()
    copies[3].wait()
    w = w_out[0]
    table[:lons, :] = dot(near[...], w).astype(jnp.bfloat16)
    inside = held[...].reshape(lats * lons, width)
    table[lons : (lats + 1) * lons, :] = dot(inside, w).astype(jnp.bfloat16)
    table[(lats + 1) * lons :, :] = dot(far[...], w).astype(jnp.bfloat16)
    copies[4].wait()
    depth = table.shape[0]
    side = (lats + 2) * HALO
    on_mate = (lon >= HALO) == (lax.rem(lax.axis_index("gy"), 2) == 0)
    edge = jnp.where(on_mate, 0, side) + lat * HALO + (lon & (HALO - 1))
    edge = jnp.where(inner, -1, edge)
    for c in range(0, edges, CHUNK):
        rows = slice(c, c + CHUNK)
        acc = dot(pick(column(src, rows), depth), table[...])
        partial[rows, :] = acc + dot(pick(column(tgt, rows), nodes), mesh_out[...])
        sides_out[rows, :] = pick(column(edge, rows), sides_out.shape[1])
    copies[5].wait()
    copies[6].wait()
    apart(indices.at[2], rows_held)
    weave(rows_held[...], beside(rows_held.shape[0]), slots_out)
    apart(indices.at[3], rows_held)
    weave(rows_held[...], in_order(rows_held.shape[0]), order_out)
    copies[7].wait()
    copies[8].wait()


def encode_kernel(
    partial, other, mate, spreading, mesh, weights, sides,
    first_out, next_out, table, messages,
):
    w = weights[0]
    tall, halo, width = mate.shape
    side = tall * halo
    table[:side, :] = dot(mate[...].reshape(side, width), w).astype(jnp.bfloat16)
    table[side : 2 * side, :] = dot(other[...].reshape(side, width), w).astype(jnp.bfloat16)
    table[2 * side :, :] = jnp.zeros((table.shape[0] - 2 * side, width), jnp.bfloat16)
    edges = partial.shape[0]
    for c in range(0, edges, CHUNK):
        rows = slice(c, c + CHUNK)
        messages[rows, :] = message(partial[rows, :] + dot(sides[rows, :], table[...]))
    summed = dot(spreading[...], messages[...])
    first = refresh(mesh[...], summed, weights[1])
    first_out[...] = first
    next_out[...] = dot(first, weights[2]).astype(jnp.bfloat16)


def request_kernel(table, upper, lower, slots, send_out, held):
    nodes = table.shape[0]
    count = slots.shape[0]
    weave(slots[...], plane_first(in_order(count), count), held)
    asked = held[...]
    lane = lax.broadcasted_iota(jnp.int32, asked.shape, 1)
    asked = asked + jnp.where((lane & (2 * CAP - 1)) >= CAP, nodes, 0)
    for c in range(0, send_out.shape[0], CHUNK):
        rows = slice(c, c + CHUNK)
        col = column(asked, rows)
        acc = dot(pick(col, nodes), table[...])
        acc = acc + dot(pick(col - nodes, nodes // 2), upper[...])
        acc = acc + dot(pick(col - nodes - nodes // 2, nodes // 2), lower[...])
        send_out[rows, :] = acc.astype(jnp.bfloat16)


def process_kernel(
    picked, target, first, w_update, w_next, second_out, table_out, messages, held, sem
):
    nodes = first.shape[0]
    tgt = target[...]
    for c in range(0, picked.shape[0], CHUNK):
        rows = slice(c, c + CHUNK)
        acc = dot(pick(column(tgt, rows), nodes), first[...])
        messages[rows, :] = message(acc + picked[rows, :].astype(jnp.float32))
    second = refresh(first[...], dot(spread(tgt, nodes), messages[...]), w_update[...])
    held[...] = second
    copy = pltpu.make_async_copy(held, second_out, sem)
    copy.start()
    table_out[...] = dot(second, w_next[...]).astype(jnp.bfloat16)
    copy.wait()


def reach_kernel(
    own, grid, source, target, w_update, partial, picks_out, spread_out, w_out, sem
):
    copy = pltpu.make_async_copy(w_update, w_out, sem)
    copy.start()
    latent = grid[...]
    cells = latent.shape[0]
    nodes = own.shape[0]
    src, tgt = source[...], target[...]
    for c in range(0, partial.shape[0], CHUNK):
        rows = slice(c, c + CHUNK)
        col = column(src, rows)
        acc = dot(pick(column(tgt, rows), cells), latent)
        partial[rows, :] = acc + dot(pick(col, nodes), own[...])
        picks_out[rows, :] = pick(col - nodes, 2 * nodes)
    spread_out[...] = spread(tgt, cells)
    copy.wait()


def decode_kernel(
    partial, other, mate, picks, spreading, grid, w_update, grid_out, messages
):
    nodes = mate.shape[0]
    for c in range(0, partial.shape[0], CHUNK):
        rows = slice(c, c + CHUNK)
        acc = partial[rows, :] + dot(picks[rows, :nodes], mate[...])
        messages[rows, :] = message(acc + dot(picks[rows, nodes:], other[...]))
    summed = dot(spreading[...], messages[...])
    grid_out[...] = refresh(grid[...], summed, w_update[...])


def on_device(
    grid_latent,
    mesh_latent,
    encode_message,
    encode_update,
    process_message,
    process_update,
    decode_message,
    decode_update,
    encode_source,
    encode_target,
    process_source,
    process_target,
    decode_source,
    decode_target,
):
    lat_rows, lon_cols, width = grid_latent.shape
    bands = lax.axis_size("gx")
    sectors = lax.axis_size("gy")
    sector = lax.axis_index("gy")
    mesh_rows = mesh_latent.reshape(-1, width)
    nodes = mesh_rows.shape[0]
    grid_rows = grid_latent.reshape(-1, width)
    cells = grid_rows.shape[0]
    edges = encode_source.size
    bf16 = jnp.bfloat16
    params = pltpu.CompilerParams(vmem_limit_bytes=40 * 1024 * 1024)
    hbm = pl.BlockSpec(memory_space=pltpu.HBM)
    vmem = pl.BlockSpec(memory_space=pltpu.VMEM)
    assert lon_cols == LON_DEV

    def pinned(array):
        return pltpu.with_memory_space_constraint(array, pltpu.HBM)

    partner = [i + 1 if i % 2 else i - 1 for i in range(max(bands, sectors))]
    far_bands = [(i, partner[i]) for i in range(1, bands - 1)]
    near_bands = [(i, i ^ 1) for i in range(bands)]
    far_sectors = [(i, partner[i] % sectors) for i in range(sectors)]
    near_sectors = [(i, i ^ 1) for i in range(sectors)]

    group = [[i for i in range(sectors) if i // HALF % 2 == h] for h in range(2)]

    every = range(sectors)
    plane_groups = [[i for i in every if i // CORES % HALF == p] for p in range(HALF)]
    columns = [i for i in every if i // CORES % PLANES == 0]
    column_groups = [[i + p * CORES for p in range(PLANES)] for i in columns]

    def exchange(array, groups):
        return lax.all_to_all(array, "gy", 0, 0, axis_index_groups=groups, tiled=True)

    band_edge = jax.ShapeDtypeStruct((lon_cols, width), bf16)
    far, near = pl.pallas_call(
        edges_kernel,
        in_specs=[hbm],
        out_specs=(vmem,) * 2,
        out_shape=(band_edge,) * 2,
        scratch_shapes=[pltpu.SemaphoreType.DMA((2,))],
        compiler_params=params,
    )(pinned(grid_latent))
    far = lax.ppermute(far, "gx", far_bands)
    near = lax.ppermute(near, "gx", near_bands)
    sector_edge = jax.ShapeDtypeStruct((lat_rows + 2, HALO, width), bf16)
    other, mate = pl.pallas_call(
        sides_kernel,
        in_specs=[vmem, hbm, vmem],
        out_specs=(vmem,) * 2,
        out_shape=(sector_edge,) * 2,
        scratch_shapes=[
            pltpu.VMEM((2, lat_rows, HALO, width), bf16),
            pltpu.SemaphoreType.DMA((2,)),
        ],
        compiler_params=params,
    )(far, pinned(grid_latent), near)
    other = lax.ppermute(other, "gy", far_sectors)
    mate = lax.ppermute(mate, "gy", near_sectors)

    tall_cells = (lat_rows + 2) * lon_cols
    depth = -(-2 * (lat_rows + 2) * HALO // LANES) * LANES
    index = jax.ShapeDtypeStruct((edges // LANES, LANES), jnp.int32)
    table_shape = jax.ShapeDtypeStruct((nodes, width), bf16)
    partial_shape = jax.ShapeDtypeStruct((edges, width), jnp.float32)
    spread_shape = jax.ShapeDtypeStruct((nodes, edges), bf16)
    rows_shape = jax.ShapeDtypeStruct((sectors // 2, LANES), jnp.int32)
    plane_shape = jax.ShapeDtypeStruct((sectors // 2 // PLANES, LANES), jnp.int32)
    partial, spreading, mesh_held, weights, sides, slots, order = pl.pallas_call(
        gather_kernel,
        in_specs=[vmem, hbm, vmem] + [hbm] * 8,
        out_specs=(vmem,) * 7,
        out_shape=(
            partial_shape,
            spread_shape,
            table_shape,
            jax.ShapeDtypeStruct((3, width, width), bf16),
            jax.ShapeDtypeStruct((edges, depth), bf16),
            plane_shape,
            index,
        ),
        scratch_shapes=[
            pltpu.VMEM((lat_rows, lon_cols, width), bf16),
            pltpu.VMEM((4, edges // LANES, LANES), jnp.int32),
            pltpu.VMEM(rows_shape.shape, jnp.int32),
            pltpu.VMEM((tall_cells, width), bf16),
            pltpu.SemaphoreType.DMA((9,)),
        ],
        compiler_params=params,
    )(
        far, pinned(grid_latent), near, pinned(mesh_rows), pinned(encode_message),
        pinned(encode_update), pinned(process_message),
        *(
            pinned(array.reshape(-1, LANES))
            for array in (encode_source, encode_target, process_source, process_target)
        ),
    )
    messages = pltpu.VMEM((edges, width), bf16)
    first, following = pl.pallas_call(
        encode_kernel,
        out_shape=(table_shape, table_shape),
        scratch_shapes=[pltpu.VMEM((depth, width), bf16), messages],
        compiler_params=params,
    )(partial, other, mate, spreading, mesh_held, weights, sides)

    following, slots = lax.optimization_barrier((following, slots))
    swapped = [(i, i ^ HALF) for i in range(sectors)]
    upper = lax.ppermute(following[: nodes // 2], "gy", swapped)
    lower = lax.ppermute(following[nodes // 2 :], "gy", swapped)
    slots = exchange(slots, plane_groups)
    slots = pl.pallas_call(planes_kernel, out_shape=rows_shape, compiler_params=params)(slots)
    slots = exchange(slots, column_groups)
    send = pl.pallas_call(
        request_kernel,
        out_shape=jax.ShapeDtypeStruct((edges, width), bf16),
        scratch_shapes=[pltpu.VMEM(index.shape, jnp.int32)],
        compiler_params=params,
    )(following, upper, lower, slots)
    picked = exchange(send.reshape(sectors // 2, -1, width), group).reshape(edges, width)
    second, table = pl.pallas_call(
        process_kernel,
        out_specs=(hbm, vmem),
        out_shape=(table_shape, table_shape),
        scratch_shapes=[
            messages, pltpu.VMEM((nodes, width), bf16), pltpu.SemaphoreType.DMA(())
        ],
        compiler_params=params,
    )(picked, order, first, process_update, decode_message)

    other = lax.ppermute(table, "gy", far_sectors)
    mate = lax.ppermute(table, "gy", near_sectors)
    source = decode_source.reshape(-1, LANES)
    owner = source // nodes % sectors
    piece = jnp.where(owner == sector, 0, jnp.where(owner == sector ^ 1, 1, 2))
    row = piece * nodes + source % nodes
    target = decode_target.reshape(-1, LANES)
    partial, picks, spreading, update = pl.pallas_call(
        reach_kernel,
        in_specs=[vmem] * 4 + [hbm],
        out_specs=(vmem,) * 4,
        out_shape=(
            partial_shape,
            jax.ShapeDtypeStruct((edges, 2 * nodes), bf16),
            jax.ShapeDtypeStruct((cells, edges), bf16),
            jax.ShapeDtypeStruct((width, width), bf16),
        ),
        scratch_shapes=[pltpu.SemaphoreType.DMA(())],
        compiler_params=params,
    )(table, grid_rows, row, target, pinned(decode_update))
    grid_output = pl.pallas_call(
        decode_kernel,
        out_shape=jax.ShapeDtypeStruct((cells, width), bf16),
        scratch_shapes=[messages],
        compiler_params=params,
    )(partial, other, mate, picks, spreading, grid_rows, update)
    return (
        grid_output.reshape(lat_rows, lon_cols, width),
        second.reshape(1, 1, nodes, width),
    )


def solution(mesh):
    edge = P("gx", "gy", None)
    return jax.shard_map(
        on_device,
        mesh=mesh,
        in_specs=(
            P("gx", "gy", None),
            P("gx", "gy", None, None),
            *([P()] * 6),
            *([edge] * 6),
        ),
        out_specs=(P("gx", "gy", None), P("gx", "gy", None, None)),
        check_vma=False,
    )
```
